768 devices in a mesh: dp: 64 (over y, x, core), mp: 12 (over z).
Axes of the slice: x: 4, y: 8, z: 12, core: 2. Of those that a mesh axis runs over, the one named last changes fastest.
Arguments:
- query_hidden: bfloat16 [3072, 4096], P('dp'), may hold values from -24 to 24
- passage_hidden: bfloat16 [3072, 4096], P('dp'), may hold values from -6 to 6
- negative_hidden: bfloat16 [21504, 4096], P('dp'), may hold values from -24 to 24
- projection: bfloat16 [4096, 3072], P(None, 'mp'), may hold values from -0.09375 to 0.09375
- positive: int32 [3072], P('dp'), may hold values from 0 to 3071, each once
- hard_ids: int32 [3072, 7], P('dp'), may hold values from 0 to 21503, as said below
Outputs:
- query_loss: float32 [3072], P('dp')
- query_grad: float32 [3072, 3072], P('dp', 'mp')
- passage_grad: float32 [3072, 3072], P('dp', 'mp')
- hard_grad: float32 [3072, 7, 3072], P('dp', None, 'mp')
The draws below stay inside these ranges and needn't reach their ends.
Inputs may be any that keep to these rules, and one draw needn't show every extreme that they name: `hard_ids`: within each block of 48 queries (one index of dp) at most 11 ids fall in the pool rows of one index of dp (id // 336); in every draw one such owner receives exactly 11 ids from every block. Each passage is the positive of exactly one query.
All inputs are finite; a program needn't handle non-finite values.
Results may differ from the reference program's by a relative error of at most 0.01.
Values may be sent and summed in bfloat16 or wider, within the bound.
No kernel may reach another device: no remote copies, remote signals or barrier semaphores. Data moves between devices by JAX's collectives and lax.ppermute only.
A program may use at most 32 MiB of HBM per device.

```python
import math
import jax
import jax.numpy as jnp
from jax import lax

H = 4096
E = 3072
HARD = 7
Q_DEV = 48
QUERIES = 3072
NEG_DEV = 336
NEG_POOL = 21504
CAP = 11


def passage_base(key):
    return jnp.clip(jax.random.normal(key, (QUERIES, H), jnp.float32), -6.0, 6.0)


def query_fresh(key):
    fresh_key = jax.random.fold_in(key, 11)
    return jnp.clip(jax.random.normal(fresh_key, (QUERIES, H), jnp.float32), -6.0, 6.0)


def hard_rows(key):
    key = jax.random.fold_in(key, 5)
    holder_list = QUERIES // Q_DEV
    request_count = Q_DEV * HARD
    position_count = holder_list * CAP
    hot_key, rest_key = jax.random.split(key)
    popular_holder = jax.random.randint(hot_key, (), 0, holder_list)

    def one_block(block_key):
        random_key_first, key_two, key_three, key_four = jax.random.split(block_key, 4)
        position_indices = jnp.arange(position_count, dtype=jnp.int32)
        position_holder = position_indices // CAP
        extra_boost = jax.random.randint(random_key_first, (holder_list,), 0, 2 ** 13)
        extra_boost = extra_boost + jnp.where(jnp.arange(holder_list) == popular_holder, 2 ** 14, 0)
        jitter_values = jax.random.randint(key_two, (position_count,), 0, 2 ** 12)
        rank_preference = (jitter_values + extra_boost[position_holder]) * position_count + position_indices
        unused, picked = lax.top_k(rank_preference, request_count)
        picked = picked[jax.random.permutation(key_three, request_count)]
        rows = jax.random.randint(key_four, (request_count,), 0, NEG_DEV)
        return (picked // CAP * NEG_DEV + rows).astype(jnp.int32).reshape(Q_DEV, HARD)
    block_keys = jax.random.split(rest_key, holder_list)
    return jax.vmap(one_block)(block_keys).reshape(QUERIES, HARD)


def draw_passage_hidden(key, part):
    base = passage_base(key)
    return base.astype(jnp.bfloat16)


def draw_query_hidden(key, part):
    fresh = query_fresh(key)
    return fresh.astype(jnp.bfloat16)


def draw_hard_ids(key, part):
    return hard_rows(key)


def draw_negative_hidden(key, part):
    chosen_rows = hard_rows(key).reshape(-1)
    fresh = query_fresh(key)
    key = jax.random.fold_in(key, 13)
    strength_key, noise_key = jax.random.split(key)
    flat_index = jnp.arange(NEG_POOL, dtype=jnp.int32)
    source = jnp.full((NEG_POOL,), NEG_POOL, jnp.int32).at[chosen_rows].min(flat_index)
    named = source < NEG_POOL
    source_query = jnp.minimum(source, NEG_POOL - 1) // HARD
    attraction = jnp.exp(jax.random.uniform(strength_key, (QUERIES,), jnp.float32, math.log(2.0), math.log(8.0))) / math.sqrt(E)
    scatter_noise = jnp.clip(jax.random.normal(noise_key, (NEG_POOL, H), jnp.float32), -6.0, 6.0)
    leaning = attraction[source_query][:, None] * fresh[source_query]
    result_rows = jnp.where(named[:, None], leaning + scatter_noise, scatter_noise)
    return result_rows.astype(jnp.bfloat16)


def shard_levels(own_key, dims, pieces, low, largest):
    loudness = 1.0
    for dim, blocks in pieces:
        heights = jax.random.uniform(jax.random.fold_in(jax.random.fold_in(own_key, 6), dim), (blocks,), jnp.float32, low / len(pieces), largest / len(pieces))
        loudness = loudness * jnp.repeat(jnp.exp(heights), dims[dim] // blocks).reshape((-1,) + (1,) * (len(dims) - 1 - dim))
    return loudness


def gaussian(key, shape, scale, most, shards=(), kind=jnp.bfloat16):
    level = shard_levels(key, shape, shards, -0.22, 0.18) if shards else 1.0
    entries = jax.random.normal(key, shape, jnp.float32) * scale * level
    return jnp.minimum(jnp.maximum(entries, -most), most).astype(kind)


def setup_inputs(seed: int = 0) -> dict:
    keys = jax.random.split(jax.random.key(seed), 7)
    query_hidden = draw_query_hidden(jax.random.fold_in(keys[6], 71), 0)
    passage_hidden = draw_passage_hidden(jax.random.fold_in(keys[6], 71), 0)
    negative_hidden = draw_negative_hidden(jax.random.fold_in(keys[6], 71), 0)
    projection = gaussian(keys[3], (H, E), H ** -0.5, 0.09375, ((1, 12),))
    positive = jax.random.permutation(keys[4], QUERIES).astype(jnp.int32)
    hard_ids = draw_hard_ids(jax.random.fold_in(keys[6], 71), 0)
    return dict(query_hidden=query_hidden, passage_hidden=passage_hidden, negative_hidden=negative_hidden, projection=projection, positive=positive, hard_ids=hard_ids)


def reference(query_hidden, passage_hidden, negative_hidden, projection, positive, hard_ids):
    score_scale = 1.0 / math.sqrt(E)
    query_emb = jnp.dot(query_hidden, projection, preferred_element_type=jnp.float32).astype(jnp.bfloat16)
    passage_emb = jnp.dot(passage_hidden, projection, preferred_element_type=jnp.float32).astype(jnp.bfloat16)
    pool_emb = jnp.dot(negative_hidden, projection, preferred_element_type=jnp.float32).astype(jnp.bfloat16)
    fetched = pool_emb[hard_ids]
    batch_scores = jnp.dot(query_emb, passage_emb.T, preferred_element_type=jnp.float32)
    hard_scores = jnp.einsum('qe,qke->qk', query_emb.astype(jnp.float32), fetched.astype(jnp.float32))
    logits = jnp.concatenate([batch_scores, hard_scores], axis=1) * score_scale
    peak = lax.optimization_barrier(jnp.max(logits, axis=1))
    expo = jnp.exp(logits - peak[:, None])
    denominator = lax.optimization_barrier(jnp.sum(expo, axis=1))
    col_index = jnp.arange(QUERIES, dtype=jnp.int32)
    target = (col_index[None, :] == positive[:, None]).astype(jnp.float32)
    pos_logit = lax.optimization_barrier(jnp.sum(target * batch_scores, axis=1)) * score_scale
    query_loss = peak + jnp.log(denominator) - pos_logit
    probs = expo / denominator[:, None]
    batch_grad = (probs[:, :QUERIES] - target).astype(jnp.bfloat16)
    hard_score_grad = probs[:, QUERIES:].astype(jnp.bfloat16)
    query_grad = jnp.dot(batch_grad, passage_emb, preferred_element_type=jnp.float32)
    query_grad = query_grad + jnp.einsum('qk,qke->qe', hard_score_grad.astype(jnp.float32), fetched.astype(jnp.float32))
    passage_grad = jnp.dot(batch_grad.T, query_emb, preferred_element_type=jnp.float32)
    hard_grad = hard_score_grad.astype(jnp.float32)[:, :, None] * query_emb.astype(jnp.float32)[:, None, :]
    return (query_loss, query_grad, passage_grad, hard_grad)
```

```python
import math

import jax
import jax.numpy as jnp
import numpy as np
from jax import lax
from jax.experimental import pallas as pl
from jax.experimental.pallas import tpu as pltpu
from jax.sharding import Mesh
from jax.sharding import PartitionSpec as P

E = 3072
SCALE = 1.0 / math.sqrt(E)
F32 = jnp.float32
BF16 = jnp.bfloat16
I32 = jnp.int32
Q = 48
K = 7
POOL = 336
CHIPS = 32
SLOT = 32
Z = 12
W = Q * CHIPS
WP = W + 128
TL, TC = W + 7, W + 8
L0 = W + 7
NEG = -3.0e38


def iota(shape, dim):
    return lax.broadcasted_iota(I32, shape, dim)


def params(mib=24):
    return pltpu.CompilerParams(vmem_limit_bytes=mib * 2**20)


def call(kernel, out, *args, flops=0, nbytes=0, **kw):
    return pl.pallas_call(
        kernel,
        out_shape=out,
        compiler_params=params(),
        cost_estimate=pl.CostEstimate(flops=flops, bytes_accessed=nbytes, transcendentals=0),
        **kw,
    )(*args)


def dot(a, b, dims=(((1,), (0,)), ((), ()))):
    return lax.dot_general(a, b, dims, preferred_element_type=F32)


def request_kernel(ids_ref, req_ref, slot_ref):
    ids = ids_ref[...]
    owner = lax.shift_right_arithmetic(ids * 49933, 25)
    row = ids - owner * (2 * POOL)
    high, low = lax.shift_right_arithmetic(row, 4).astype(F32), (row & 15).astype(F32)
    marks = jnp.where(owner[None] == iota((CHIPS, 8, 128), 0), 1.0, 0.0)
    flat = marks.reshape(CHIPS * 8, 128).astype(BF16)
    upper = jnp.where(iota((128, 128), 0) < iota((128, 128), 1), 1.0, 0.0).astype(BF16)
    a, b = iota((256, 256), 0), iota((256, 256), 1)
    lower = jnp.where((b < a) & (lax.shift_right_logical(a, 3) == lax.shift_right_logical(b, 3)), 1.0, 0.0).astype(BF16)
    above = dot(lower, flat).astype(BF16)
    before = dot(flat, upper) + dot(above, jnp.ones((128, 128), BF16))
    rank = jnp.sum(marks * before.reshape(CHIPS, 8, 128), axis=0)
    rank_cols = rank.T
    lanes = iota((128, 128), 1).astype(F32)
    total = jnp.zeros((2 * CHIPS, 128), F32)
    for k in range(K):
        mine = owner[k : k + 1, :] == iota((CHIPS, 128), 0)
        left = jnp.concatenate(
            [jnp.where(mine, high[k : k + 1, :], 0.0), jnp.where(mine, low[k : k + 1, :], 0.0)], axis=0
        )
        right = jnp.where(rank_cols[:, k : k + 1] == lanes, 1.0, 0.0)
        total += dot(left.astype(BF16), right.astype(BF16))
    request = (total[:CHIPS] * 16.0 + total[CHIPS:]).astype(I32)
    req_ref[...] = jnp.broadcast_to(request[:, None, :], (CHIPS, 8, 128))
    slot_ref[...] = (owner.astype(F32) * SLOT + rank).T


def project_kernel(qh_ref, ph_ref, nh_ref, w_ref, pos_ref, emb_ref, pass_ref, acc):
    step = pl.program_id(0)

    @pl.when(step == 0)
    def _():
        acc[...] = jnp.zeros_like(acc)

    w = w_ref[...]
    acc[0:Q] += dot(qh_ref[...], w)
    acc[Q : 2 * Q] += dot(ph_ref[...], w)
    acc[2 * Q :] += dot(nh_ref[...], w)

    @pl.when(step == pl.num_programs(0) - 1)
    def _():
        emb_ref[0 : 2 * Q + POOL] = acc[...].astype(BF16)
        pass_ref[...] = jnp.broadcast_to(acc[Q : 2 * Q].astype(BF16)[None], (CHIPS, Q, 256))
        pos = jnp.broadcast_to(pos_ref[...], (16, 256))
        high = lax.shift_right_arithmetic(pos, 6).astype(F32)
        low = (pos & 63).astype(F32)
        emb_ref[2 * Q + POOL :] = jnp.where(iota((16, 256), 0) == 0, high, low).astype(BF16)


def answer_kernel(core_ref, asked_ref, emb_ref, other_ref, send_ref, both_ref, pool):
    core = core_ref[0]
    pool[0:POOL] = emb_ref[2 * Q : 2 * Q + POOL]
    pool[POOL : 2 * POOL] = other_ref[2 * Q : 2 * Q + POOL]
    pool[2 * POOL :] = jnp.zeros((768 - 2 * POOL, 256), BF16)
    first = core == 0

    @pl.when(first)
    def _():
        both_ref[0:Q] = emb_ref[0:Q]
        both_ref[Q:] = other_ref[0:Q]

    @pl.when(jnp.logical_not(first))
    def _():
        both_ref[0:Q] = other_ref[0:Q]
        both_ref[Q:] = emb_ref[0:Q]

    asked = asked_ref[:, 0, :]
    flipped = jnp.where(asked >= POOL, asked - POOL, asked + POOL)
    wanted = jnp.where(core == 1, flipped, asked).astype(F32).T
    lanes = iota((SLOT, 768), 1).astype(F32)
    rows = pool[...]
    for g in range(CHIPS // 4):
        hot = jnp.concatenate(
            [jnp.where(wanted[0:SLOT, j : j + 1] == lanes, 1.0, 0.0) for j in range(4 * g, 4 * g + 4)], axis=0
        )
        found = dot(hot.astype(BF16), rows).astype(BF16)
        for i in range(4):
            send_ref[4 * g + i] = found[SLOT * i : SLOT * (i + 1)]


def score_kernel(both_ref, pass_ref, part_ref):
    queries = both_ref[...]
    for g in range(4):
        block = pass_ref[8 * g : 8 * g + 8].reshape(8 * Q, 256)
        part_ref[:, 8 * Q * g : 8 * Q * (g + 1)] = dot(queries, block, (((1,), (1,)), ((), ())))


def hard_kernel(core_ref, part_ref, rows_ref, emb_ref, other_ref, slot_ref, send_ref, fetched_ref):
    first = core_ref[0] == 0
    mine = emb_ref[0:Q]
    send_ref[:, 0:W] = part_ref[...]
    rows = rows_ref[...].reshape(CHIPS * SLOT, 256)
    places = iota((Q, CHIPS * SLOT), 1).astype(F32)
    slots = slot_ref[...]
    hot = jnp.concatenate([jnp.where(slots[0:Q, k : k + 1] == places, 1.0, 0.0) for k in range(K)], axis=0)
    found = dot(hot.astype(BF16), rows)
    lane = iota((Q, 128), 1)
    mine32 = mine.astype(F32)
    hard = jnp.zeros((Q, 128), F32)
    for k in range(K):
        row = found[Q * k : Q * (k + 1)]
        fetched_ref[k] = row.astype(BF16)
        hard = jnp.where(lane == k, jnp.sum(mine32 * row, axis=1, keepdims=True), hard)

    def target(ref):
        pos = ref[2 * Q + POOL :].astype(F32).T
        pos = (pos[0:Q, 0:1] * 64.0 + pos[0:Q, 1:2]).astype(I32)
        index = pos.astype(F32) + 0.5
        chip = (index * (1.0 / 96.0)).astype(I32)
        dp = (index * (1.0 / 48.0)).astype(I32)
        column = (chip * Q + pos - dp * Q).astype(F32)
        return jnp.where(lane == 7, column, jnp.where(lane == 8, (dp - 2 * chip).astype(F32), 0.0))

    mine_extra, other_extra = hard + target(emb_ref), target(other_ref)
    send_ref[0:Q, W:] = jnp.where(first, mine_extra, other_extra)
    send_ref[Q:, W:] = jnp.where(first, other_extra, mine_extra)


def stats_kernel(core_ref, part_ref, logit_ref, stat_ref):
    core = core_ref[0]
    z = core_ref[1]
    own = (z >= Z // 2) == (core == 1)
    total = part_ref[0]
    for i in range(1, Z):
        total += part_ref[i]
    lane = iota((8, WP), 1)
    valid = (lane < W) | (own & (lane < W + K))
    logits = jnp.where(valid, total * SCALE, NEG)
    peak = jnp.max(logits, axis=1, keepdims=True)
    mass = jnp.sum(jnp.where(valid, jnp.exp(logits - peak), 0.0), axis=1, keepdims=True)
    column = part_ref[0, :, TL : TL + 1]
    here = part_ref[0, :, TC : TC + 1] == core.astype(F32)
    column = jnp.where(here, column, -1.0)
    aim = lane.astype(F32) == column
    hit = jnp.sum(jnp.where(aim, logits, 0.0), axis=1, keepdims=True)
    logit_ref[...] = logits
    lane = iota((8, 128), 1)
    stat_ref[...] = jnp.where(
        lane == 0, peak, jnp.where(lane == 1, mass, jnp.where(lane == 2, hit, jnp.where(lane == 3, column, 0.0)))
    )


def grad_kernel(logit_ref, mine_ref, other_ref, send_ref):
    mine, other = mine_ref[...], other_ref[...]
    peak = jnp.maximum(mine[:, 0:1], other[:, 0:1])
    mass = mine[:, 1:2] * jnp.exp(mine[:, 0:1] - peak) + other[:, 1:2] * jnp.exp(other[:, 0:1] - peak)
    loss = peak + jnp.log(mass) - (mine[:, 2:3] + other[:, 2:3])
    logits = logit_ref[...]
    lane = iota((8, WP), 1)
    probs = jnp.where(logits > NEG, jnp.exp(logits - peak) / mass, 0.0)
    grads = probs - jnp.where(lane.astype(F32) == mine[:, 3:4], 1.0, 0.0)
    high = loss.astype(BF16).astype(F32)
    mid = (loss - high).astype(BF16).astype(F32)
    low = loss - high - mid
    grads = jnp.where(lane == L0, high, jnp.where(lane == L0 + 1, mid, jnp.where(lane == L0 + 2, low, grads)))
    send_ref[...] = jnp.broadcast_to(grads.astype(BF16)[None], (Z, 8, WP))


def turn_kernel(grad_ref, both_ref, send_ref, flat_ref):
    grads = grad_ref[...].astype(F32).reshape(Z * 8, WP).astype(BF16)
    flat_ref[...] = grads
    queries = both_ref[...]
    for g in range(4):
        part = dot(grads[:, 8 * Q * g : 8 * Q * (g + 1)], queries, (((0,), (0,)), ((), ())))
        send_ref[8 * g : 8 * g + 8] = part.astype(BF16).reshape(8, Q, 256)


def query_kernel(core_ref, grad_ref, recv_ref, fetched_ref, emb_ref, mine_ref, other_ref, hard_ref, loss_ref):
    first = core_ref[0] == 0
    total = jnp.zeros((2 * Q, 256), F32)
    for g in range(4):
        block = recv_ref[8 * g : 8 * g + 8].reshape(8 * Q, 256)
        total += dot(grad_ref[:, 8 * Q * g : 8 * Q * (g + 1)], block)
    upper, lower = total[0:Q], total[Q:]
    other_ref[...] = jnp.where(first, lower, upper)
    tail = grad_ref[:, W:].astype(F32)
    mine = jnp.where(first, tail[0:Q], tail[Q:])
    queries = emb_ref[0:Q].astype(F32)
    result = jnp.where(first, upper, lower)
    for k in range(K):
        weight = mine[:, k : k + 1]
        result += weight * fetched_ref[k].astype(F32)
        hard_ref[k] = weight * queries
    mine_ref[...] = result
    loss = mine[:, K : K + 1] + mine[:, K + 1 : K + 2] + mine[:, K + 2 : K + 3]
    loss_ref[...] = jnp.broadcast_to(loss, (Q, 128)).T[0:8]


def passage_kernel(parts_ref, mine_ref, other_ref, out_ref, query_ref):
    total = parts_ref[0].astype(F32)
    for j in range(1, CHIPS):
        total += parts_ref[j].astype(F32)
    out_ref[...] = total
    query_ref[...] = mine_ref[...] + other_ref[...]


def swap(x):
    return lax.ppermute(x, "c", [(0, 1), (1, 0)])


def exchange(x, axes):
    return lax.all_to_all(x, axes, split_axis=0, concat_axis=0, tiled=True)


def shape(dims, dtype):
    return jax.ShapeDtypeStruct(dims, dtype)


SMEM = pl.BlockSpec(memory_space=pltpu.SMEM)
VMEM = pl.BlockSpec(memory_space=pltpu.VMEM)


def local(query_hidden, passage_hidden, negative_hidden, projection, positive, hard_ids):
    place = jnp.stack([lax.axis_index("c"), lax.axis_index("z")]).astype(I32)
    ids = jnp.pad(hard_ids.T, ((0, 1), (0, 128 - Q)), constant_values=-1)
    request, slots = call(request_kernel, (shape((CHIPS, 8, 128), I32), shape((128, 8), F32)), ids)
    asked = exchange(request, ("y", "x"))

    steps = 8
    depth = query_hidden.shape[1] // steps
    pos = jnp.pad(positive[None, :], ((0, 0), (0, 256 - Q)))
    emb, passages = call(
        project_kernel,
        (shape((2 * Q + POOL + 16, 256), BF16), shape((CHIPS, Q, 256), BF16)),
        query_hidden,
        passage_hidden,
        negative_hidden,
        projection,
        pos,
        grid=(steps,),
        in_specs=[
            pl.BlockSpec((Q, depth), lambda i: (0, i)),
            pl.BlockSpec((Q, depth), lambda i: (0, i)),
            pl.BlockSpec((POOL, depth), lambda i: (0, i)),
            pl.BlockSpec((depth, 256), lambda i: (i, 0)),
            pl.BlockSpec((1, 256), lambda i: (0, 0)),
        ],
        out_specs=[
            pl.BlockSpec((2 * Q + POOL + 16, 256), lambda i: (0, 0)),
            pl.BlockSpec((CHIPS, Q, 256), lambda i: (0, 0, 0)),
        ],
        scratch_shapes=[pltpu.VMEM((2 * Q + POOL, 256), F32)],
        flops=2 * 432 * 4096 * 256,
        nbytes=6 * 2**20,
    )
    other = swap(emb)
    passages, asked = lax.optimization_barrier((passages, asked))
    recv = exchange(passages, ("y", "x"))
    answers, both = call(
        answer_kernel,
        (shape((CHIPS, SLOT, 256), BF16), shape((2 * Q, 256), BF16)),
        place,
        asked,
        emb,
        other,
        in_specs=[SMEM, VMEM, VMEM, VMEM],
        scratch_shapes=[pltpu.VMEM((768, 256), BF16)],
        flops=2 * 1024 * 768 * 256,
        nbytes=2 * 2**20,
    )
    answers, recv = lax.optimization_barrier((answers, recv))
    rows = exchange(answers, ("y", "x"))
    part = call(
        score_kernel, shape((2 * Q, W), F32), both, recv, flops=2 * 96 * 1536 * 256, nbytes=2 * 2**20
    )
    send, fetched = call(
        hard_kernel,
        (shape((2 * Q, WP), F32), shape((K, Q, 256), BF16)),
        place,
        part,
        rows,
        emb,
        other,
        slots,
        in_specs=[SMEM, VMEM, VMEM, VMEM, VMEM, VMEM],
        flops=2 * 336 * 1024 * 256,
        nbytes=3 * 2**20,
    )
    parts = exchange(send.reshape(Z, 8, WP), "z")
    logits, stat = call(
        stats_kernel,
        (shape((8, WP), F32), shape((8, 128), F32)),
        place,
        parts,
        in_specs=[SMEM, VMEM],
        nbytes=2**20,
    )
    stat_other = swap(stat)
    grads = exchange(call(grad_kernel, shape((Z, 8, WP), BF16), logits, stat, stat_other, nbytes=2**19), "z")
    sums, flat = call(
        turn_kernel,
        (shape((CHIPS, Q, 256), BF16), shape((Z * 8, WP), BF16)),
        grads,
        both,
        flops=2 * 96 * 1536 * 256,
        nbytes=2 * 2**20,
    )
    sums = exchange(sums, ("y", "x"))
    query_mine, query_other, hard_grad, loss = call(
        query_kernel,
        (shape((Q, 256), F32), shape((Q, 256), F32), shape((K, Q, 256), F32), shape((8, Q), F32)),
        place,
        flat,
        recv,
        fetched,
        emb,
        in_specs=[SMEM, VMEM, VMEM, VMEM, VMEM],
        flops=2 * 96 * 1536 * 256,
        nbytes=3 * 2**20,
    )
    query_back = swap(query_other)
    passage_grad, query_grad = call(
        passage_kernel,
        (shape((Q, 256), F32), shape((Q, 256), F32)),
        sums,
        query_mine,
        query_back,
        nbytes=2**20,
    )
    return (loss[0], query_grad, passage_grad, jnp.transpose(hard_grad, (1, 0, 2)))


def solution(mesh):
    devices = np.asarray(mesh.devices)
    view = Mesh(devices.reshape(8, 4, 2, Z), ("y", "x", "c", "z"))
    dp = ("y", "x", "c")
    return jax.shard_map(
        local,
        mesh=view,
        in_specs=(P(dp, None), P(dp, None), P(dp, None), P(None, "z"), P(dp), P(dp, None)),
        out_specs=(P(dp), P(dp, "z"), P(dp, "z"), P(dp, None, "z")),
        check_vma=False,
    )
```

```python
import math

import jax
import jax.numpy as jnp
import numpy as np
from jax import lax
from jax.experimental import pallas as pl
from jax.experimental.pallas import tpu as pltpu
from jax.sharding import Mesh
from jax.sharding import PartitionSpec as P

E = 3072
SCALE = 1.0 / math.sqrt(E)
F32 = jnp.float32
BF16 = jnp.bfloat16
I32 = jnp.int32
Q = 48
K = 7
POOL = 336
X, Y, Z = 4, 8, 12
CHIPS = X * Y
SLOT = 24
W = Q * CHIPS
H = W // 2
WP = W + 128
PASS = Y * Q
L0 = W + 7
NEG = -3.0e38
STEP = 8.0
TOP = 32700.0
TCOL, TCORE, ESCORE, EHARD = 7, 8, 9, 10


def iota(shape, dim):
    return lax.broadcasted_iota(I32, shape, dim)


def params(mib=24):
    return pltpu.CompilerParams(vmem_limit_bytes=mib * 2**20)


def call(kernel, out, *args, flops=0, nbytes=0, **kw):
    return pl.pallas_call(
        kernel,
        out_shape=out,
        compiler_params=params(),
        cost_estimate=pl.CostEstimate(flops=flops, bytes_accessed=nbytes, transcendentals=0),
        **kw,
    )(*args)


def dot(a, b, dims=(((1,), (0,)), ((), ()))):
    return lax.dot_general(a, b, dims, preferred_element_type=F32)


def requests(ids):
    owner = lax.shift_right_arithmetic(ids * 49933, 25)
    row = ids - owner * (2 * POOL)
    high, low = lax.shift_right_arithmetic(row, 4).astype(F32), (row & 15).astype(F32)
    marks = jnp.where(owner[None] == iota((CHIPS, 8, 128), 0), 1.0, 0.0)
    flat = marks.reshape(CHIPS * 8, 128).astype(BF16)
    upper = jnp.where(iota((128, 128), 0) < iota((128, 128), 1), 1.0, 0.0).astype(BF16)
    a, b = iota((256, 256), 0), iota((256, 256), 1)
    lower = jnp.where((b < a) & (lax.shift_right_logical(a, 3) == lax.shift_right_logical(b, 3)), 1.0, 0.0).astype(BF16)
    above = dot(lower, flat).astype(BF16)
    before = dot(flat, upper) + dot(above, jnp.ones((128, 128), BF16))
    rank = jnp.sum(marks * before.reshape(CHIPS, 8, 128), axis=0)
    x, y = owner & 3, lax.shift_right_arithmetic(owner, 2)
    places = (x.astype(F32) * 32.0 + rank).T
    lanes = iota((128, 128), 1).astype(F32)
    total = jnp.zeros((2 * Y, 128), F32)
    for k in range(K):
        mine = y[k : k + 1, :] == iota((Y, 128), 0)
        left = jnp.concatenate(
            [jnp.where(mine, high[k : k + 1, :], 0.0), jnp.where(mine, low[k : k + 1, :], 0.0)], axis=0
        )
        right = jnp.where(places[:, k : k + 1] == lanes, 1.0, 0.0)
        total += dot(left.astype(BF16), right.astype(BF16))
    slots = ((x * Y + y).astype(F32) * SLOT + rank).T
    return total, slots


def passage_project_kernel(ids_ref, ph_ref, w_ref, send_ref, slot_ref, acc, wanted):
    step = pl.program_id(0)

    @pl.when(step == 0)
    def _():
        acc[...] = jnp.zeros_like(acc)
        total, slots = requests(ids_ref[...])
        slot_ref[...] = slots
        wanted[:, 0:128] = total
        wanted[:, 128:] = jnp.zeros((2 * Y, 128), F32)

    acc[...] += dot(ph_ref[...], w_ref[...])

    @pl.when(step == pl.num_programs(0) - 1)
    def _():
        passages = acc[...].astype(BF16)
        line = iota((16, 256), 0)
        for y in range(Y):
            send_ref[y, 0:Q] = passages
            parts = jnp.where(line == 0, wanted[y : y + 1], jnp.where(line == 1, wanted[Y + y : Y + y + 1], 0.0))
            send_ref[y, Q:] = parts.astype(BF16)


def project_kernel(qh_ref, nh_ref, w_ref, pos_ref, emb_ref, acc):
    step = pl.program_id(0)

    @pl.when(step == 0)
    def _():
        acc[...] = jnp.zeros_like(acc)

    w = w_ref[...]
    acc[0:Q] += dot(qh_ref[...], w)
    acc[Q:] += dot(nh_ref[...], w)

    @pl.when(step == pl.num_programs(0) - 1)
    def _():
        emb_ref[0 : Q + POOL] = acc[...].astype(BF16)
        pos = jnp.broadcast_to(pos_ref[...], (16, 256))
        high = lax.shift_right_arithmetic(pos, 6).astype(F32)
        low = (pos & 63).astype(F32)
        emb_ref[Q + POOL :] = jnp.where(iota((16, 256), 0) == 0, high, low).astype(BF16)


def relay_kernel(recv_ref, send_ref):
    block = recv_ref[:, 0:Q].reshape(PASS, 256)
    tail = recv_ref[:, Q:].astype(F32)
    high, low = tail[:, 0, 0:128], tail[:, 1, 0:128]
    both = jnp.concatenate([high, low], axis=0)
    for x in range(X):
        send_ref[x, 0:PASS] = block
        part = jnp.concatenate([both[:, 32 * x : 32 * x + 32], jnp.zeros((2 * Y, 224), F32)], axis=1)
        send_ref[x, PASS:] = part.astype(BF16)


def answer_kernel(core_ref, recv_ref, emb_ref, other_ref, send_ref, both_ref, pool):
    core = core_ref[0]
    pool[0:POOL] = emb_ref[Q : Q + POOL]
    pool[POOL : 2 * POOL] = other_ref[Q : Q + POOL]
    pool[2 * POOL :] = jnp.zeros((768 - 2 * POOL, 256), BF16)
    first = core == 0

    @pl.when(first)
    def _():
        both_ref[0:Q] = emb_ref[0:Q]
        both_ref[Q:] = other_ref[0:Q]

    @pl.when(jnp.logical_not(first))
    def _():
        both_ref[0:Q] = other_ref[0:Q]
        both_ref[Q:] = emb_ref[0:Q]

    lanes = iota((SLOT, 768), 1).astype(F32)
    rows = pool[...]
    for x in range(X):
        parts = recv_ref[x, PASS:].astype(F32)
        asked = parts[0:Y, 0:128] * 16.0 + parts[Y:, 0:128]
        flipped = jnp.where(asked >= POOL, asked - POOL, asked + POOL)
        wanted = jnp.where(core == 1, flipped, asked).T
        hot = jnp.concatenate([jnp.where(wanted[0:SLOT, y : y + 1] == lanes, 1.0, 0.0) for y in range(Y)], axis=0)
        found = dot(hot.astype(BF16), rows)
        left = found[:, 0:128].reshape(Y, SLOT, 128)
        right = found[:, 128:].reshape(Y, SLOT, 128)
        send_ref[Y * x : Y * (x + 1)] = jnp.concatenate([left, right], axis=1).astype(BF16)


def score_kernel(both_ref, pass_ref, part_ref):
    queries = both_ref[...]
    for x in range(X):
        part_ref[:, PASS * x : PASS * (x + 1)] = dot(queries, pass_ref[x, 0:PASS], (((1,), (1,)), ((), ())))


def quantize(values):
    most = jnp.maximum(jnp.max(jnp.abs(values), axis=1, keepdims=True), 1e-30)
    power = jnp.ceil(jnp.log2(most) * STEP + 0.02)
    return jnp.floor(values * (TOP * jnp.exp2(power * (-1.0 / STEP))) + 0.5), power


def hard_kernel(core_ref, part_ref, rows_ref, emb_ref, other_ref, slot_ref, send_ref, fetched_ref):
    first = core_ref[0] == 0
    mine = emb_ref[0:Q]
    got = rows_ref[...].astype(F32)
    left = got[:, 0:SLOT].reshape(CHIPS * SLOT, 128)
    right = got[:, SLOT:].reshape(CHIPS * SLOT, 128)
    rows = jnp.concatenate([left, right], axis=1).astype(BF16)
    places = iota((Q, CHIPS * SLOT), 1).astype(F32)
    slots = slot_ref[...]
    hot = jnp.concatenate([jnp.where(slots[0:Q, k : k + 1] == places, 1.0, 0.0) for k in range(K)], axis=0)
    found = dot(hot.astype(BF16), rows)
    lane = iota((Q, 128), 1)
    mine32 = mine.astype(F32)
    hard = jnp.zeros((Q, 128), F32)
    for k in range(K):
        row = found[Q * k : Q * (k + 1)]
        fetched_ref[k] = row.astype(BF16)
        hard = jnp.where(lane == k, jnp.sum(mine32 * row, axis=1, keepdims=True), hard)
    hard, power = quantize(hard)
    hard = jnp.where(lane == EHARD, power, hard)

    def target(ref):
        pos = ref[Q + POOL :].astype(F32).T
        pos = (pos[0:Q, 0:1] * 64.0 + pos[0:Q, 1:2]).astype(I32)
        index = pos.astype(F32) + 0.5
        chip = (index * (1.0 / 96.0)).astype(I32)
        dp = (index * (1.0 / 48.0)).astype(I32)
        place = (chip & 3) * Y + lax.shift_right_arithmetic(chip, 2)
        column = (place * Q + pos - dp * Q).astype(F32)
        return jnp.where(lane == TCOL, column, jnp.where(lane == TCORE, (dp - 2 * chip).astype(F32), 0.0))

    mine_extra, other_extra = hard + target(emb_ref), target(other_ref)
    extra = jnp.concatenate(
        [jnp.where(first, mine_extra, other_extra), jnp.where(first, other_extra, mine_extra)], axis=0
    )
    scores, power = quantize(part_ref[...])
    extra = jnp.where(iota((2 * Q, 128), 1) == ESCORE, power, extra)
    left = jnp.concatenate([scores[:, 0:H], extra], axis=1).reshape(Z, 8, H + 128)
    right = jnp.concatenate([scores[:, H:], jnp.zeros((2 * Q, 128), F32)], axis=1).reshape(Z, 8, H + 128)
    send_ref[...] = jnp.concatenate([left, right], axis=1).astype(I32).astype(jnp.int16)


def stats_kernel(core_ref, part_ref, logit_ref, stat_ref):
    core = core_ref[0]
    z = core_ref[1]
    own = (z >= Z // 2) == (core == 1)
    left = jnp.zeros((8, H), F32)
    right = jnp.zeros((8, H), F32)
    hard = jnp.zeros((8, 128), F32)
    for i in range(Z):
        part = part_ref[i].astype(I32).astype(F32)
        extra = part[0:8, H:]
        scale = jnp.exp2(extra[:, ESCORE : ESCORE + 1] * (1.0 / STEP)) * (SCALE / TOP)
        left += part[0:8, 0:H] * scale
        right += part[8:16, 0:H] * scale
        hard += extra * (jnp.exp2(extra[:, EHARD : EHARD + 1] * (1.0 / STEP)) * (SCALE / TOP))
    lane = iota((8, 128), 1)
    hard = jnp.where(own & (lane < K), hard, NEG)
    logits = jnp.concatenate([left, right, hard], axis=1)
    peak = jnp.max(logits, axis=1, keepdims=True)
    mass = jnp.sum(jnp.where(logits > NEG, jnp.exp(logits - peak), 0.0), axis=1, keepdims=True)
    column = jnp.where(extra[:, TCORE : TCORE + 1] == core.astype(F32), extra[:, TCOL : TCOL + 1], -1.0)
    aim = iota((8, WP), 1).astype(F32) == column
    hit = jnp.sum(jnp.where(aim, logits, 0.0), axis=1, keepdims=True)
    logit_ref[...] = logits
    stat_ref[...] = jnp.where(
        lane == 0, peak, jnp.where(lane == 1, mass, jnp.where(lane == 2, hit, jnp.where(lane == 3, column, 0.0)))
    )


def grad_kernel(logit_ref, mine_ref, other_ref, send_ref):
    mine, other = mine_ref[...], other_ref[...]
    peak = jnp.maximum(mine[:, 0:1], other[:, 0:1])
    mass = mine[:, 1:2] * jnp.exp(mine[:, 0:1] - peak) + other[:, 1:2] * jnp.exp(other[:, 0:1] - peak)
    loss = peak + jnp.log(mass) - (mine[:, 2:3] + other[:, 2:3])
    logits = logit_ref[...]
    lane = iota((8, WP), 1)
    probs = jnp.where(logits > NEG, jnp.exp(logits - peak) / mass, 0.0)
    grads = probs - jnp.where(lane.astype(F32) == mine[:, 3:4], 1.0, 0.0)
    high = loss.astype(BF16).astype(F32)
    mid = (loss - high).astype(BF16).astype(F32)
    low = loss - high - mid
    grads = jnp.where(lane == L0, high, jnp.where(lane == L0 + 1, mid, jnp.where(lane == L0 + 2, low, grads)))
    send_ref[...] = jnp.broadcast_to(grads.astype(BF16)[None], (Z, 8, WP))


def turn_kernel(grad_ref, both_ref, send_ref, flat_ref):
    grads = grad_ref[...].astype(F32).reshape(Z * 8, WP).astype(BF16)
    flat_ref[...] = grads
    queries = both_ref[...]
    for x in range(X):
        part = dot(grads[:, PASS * x : PASS * (x + 1)], queries, (((0,), (0,)), ((), ())))
        send_ref[Y * x : Y * (x + 1)] = part.astype(BF16).reshape(Y, Q, 256)


def query_kernel(core_ref, grad_ref, recv_ref, fetched_ref, emb_ref, mine_ref, other_ref, hard_ref, loss_ref):
    first = core_ref[0] == 0
    total = jnp.zeros((2 * Q, 256), F32)
    for x in range(X):
        total += dot(grad_ref[:, PASS * x : PASS * (x + 1)], recv_ref[x, 0:PASS])
    upper, lower = total[0:Q], total[Q:]
    other_ref[...] = jnp.where(first, lower, upper)
    tail = grad_ref[:, W:].astype(F32)
    mine = jnp.where(first, tail[0:Q], tail[Q:])
    queries = emb_ref[0:Q].astype(F32)
    result = jnp.where(first, upper, lower)
    for k in range(K):
        weight = mine[:, k : k + 1]
        result += weight * fetched_ref[k].astype(F32)
        hard_ref[k] = weight * queries
    mine_ref[...] = result
    loss = mine[:, K : K + 1] + mine[:, K + 1 : K + 2] + mine[:, K + 2 : K + 3]
    loss_ref[...] = jnp.broadcast_to(loss, (Q, 128)).T[0:8]


def passage_kernel(parts_ref, mine_ref, other_ref, out_ref, query_ref):
    total = parts_ref[0].astype(F32)
    for j in range(1, CHIPS):
        total += parts_ref[j].astype(F32)
    out_ref[...] = total
    query_ref[...] = mine_ref[...] + other_ref[...]


def swap(x):
    return lax.ppermute(x, "c", [(0, 1), (1, 0)])


def exchange(x, axes):
    return lax.all_to_all(x, axes, split_axis=0, concat_axis=0, tiled=True)


def shape(dims, dtype):
    return jax.ShapeDtypeStruct(dims, dtype)


SMEM = pl.BlockSpec(memory_space=pltpu.SMEM)
VMEM = pl.BlockSpec(memory_space=pltpu.VMEM)


def local(query_hidden, passage_hidden, negative_hidden, projection, positive, hard_ids):
    place = jnp.stack([lax.axis_index("c"), lax.axis_index("z")]).astype(I32)
    ids = jnp.pad(hard_ids.T, ((0, 1), (0, 128 - Q)), constant_values=-1)
    pos = jnp.pad(positive[None, :], ((0, 0), (0, 256 - Q)))
    steps = 4
    depth = query_hidden.shape[1] // steps
    send, slots = call(
        passage_project_kernel,
        (shape((Y, Q + 16, 256), BF16), shape((128, 8), F32)),
        ids,
        passage_hidden,
        projection,
        grid=(steps,),
        in_specs=[
            pl.BlockSpec((8, 128), lambda i: (0, 0)),
            pl.BlockSpec((Q, depth), lambda i: (0, i)),
            pl.BlockSpec((depth, 256), lambda i: (i, 0)),
        ],
        out_specs=[
            pl.BlockSpec((Y, Q + 16, 256), lambda i: (0, 0, 0)),
            pl.BlockSpec((128, 8), lambda i: (0, 0)),
        ],
        scratch_shapes=[pltpu.VMEM((Q, 256), F32), pltpu.VMEM((2 * Y, 256), F32)],
        flops=2 * 48 * 4096 * 256,
        nbytes=3 * 2**20,
    )
    row = exchange(send, "y")
    emb = call(
        project_kernel,
        shape((Q + POOL + 16, 256), BF16),
        query_hidden,
        negative_hidden,
        projection,
        pos,
        grid=(steps,),
        in_specs=[
            pl.BlockSpec((Q, depth), lambda i: (0, i)),
            pl.BlockSpec((POOL, depth), lambda i: (0, i)),
            pl.BlockSpec((depth, 256), lambda i: (i, 0)),
            pl.BlockSpec((1, 256), lambda i: (0, 0)),
        ],
        out_specs=pl.BlockSpec((Q + POOL + 16, 256), lambda i: (0, 0)),
        scratch_shapes=[pltpu.VMEM((Q + POOL, 256), F32)],
        flops=2 * 384 * 4096 * 256,
        nbytes=6 * 2**20,
    )
    other = swap(emb)
    recv = exchange(call(relay_kernel, shape((X, PASS + 16, 256), BF16), row, nbytes=2**20), "x")
    answers, both = call(
        answer_kernel,
        (shape((CHIPS, 2 * SLOT, 128), BF16), shape((2 * Q, 256), BF16)),
        place,
        recv,
        emb,
        other,
        in_specs=[SMEM, VMEM, VMEM, VMEM],
        scratch_shapes=[pltpu.VMEM((768, 256), BF16)],
        flops=2 * 768 * 768 * 256,
        nbytes=2 * 2**20,
    )
    rows = exchange(answers, ("x", "y"))
    part = call(
        score_kernel, shape((2 * Q, W), F32), both, recv, flops=2 * 96 * 1536 * 256, nbytes=2 * 2**20
    )
    send, fetched = call(
        hard_kernel,
        (shape((Z, 16, H + 128), jnp.int16), shape((K, Q, 256), BF16)),
        place,
        part,
        rows,
        emb,
        other,
        slots,
        in_specs=[SMEM, VMEM, VMEM, VMEM, VMEM, VMEM],
        flops=2 * 336 * 1024 * 256,
        nbytes=3 * 2**20,
    )
    parts = exchange(send, "z")
    logits, stat = call(
        stats_kernel,
        (shape((8, WP), F32), shape((8, 128), F32)),
        place,
        parts,
        in_specs=[SMEM, VMEM],
        nbytes=2**20,
    )
    stat_other = swap(stat)
    grads = exchange(call(grad_kernel, shape((Z, 8, WP), BF16), logits, stat, stat_other, nbytes=2**19), "z")
    sums, flat = call(
        turn_kernel,
        (shape((CHIPS, Q, 256), BF16), shape((Z * 8, WP), BF16)),
        grads,
        both,
        flops=2 * 96 * 1536 * 256,
        nbytes=2 * 2**20,
    )
    sums = exchange(sums, ("x", "y"))
    query_mine, query_other, hard_grad, loss = call(
        query_kernel,
        (shape((Q, 256), F32), shape((Q, 256), F32), shape((K, Q, 256), F32), shape((8, Q), F32)),
        place,
        flat,
        recv,
        fetched,
        emb,
        in_specs=[SMEM, VMEM, VMEM, VMEM, VMEM],
        flops=2 * 96 * 1536 * 256,
        nbytes=3 * 2**20,
    )
    query_back = swap(query_other)
    passage_grad, query_grad = call(
        passage_kernel,
        (shape((Q, 256), F32), shape((Q, 256), F32)),
        sums,
        query_mine,
        query_back,
        nbytes=2**20,
    )
    return (loss[0], query_grad, passage_grad, jnp.transpose(hard_grad, (1, 0, 2)))


def solution(mesh):
    devices = np.asarray(mesh.devices)
    view = Mesh(devices.reshape(Y, X, 2, Z), ("y", "x", "c", "z"))
    dp = ("y", "x", "c")
    return jax.shard_map(
        local,
        mesh=view,
        in_specs=(P(dp, None), P(dp, None), P(dp, None), P(None, "z"), P(dp), P(dp, None)),
        out_specs=(P(dp), P(dp, "z"), P(dp, "z"), P(dp, None, "z")),
        check_vma=False,
    )
```

```python
import math

import jax
import jax.numpy as jnp
import numpy as np
from jax import lax
from jax.experimental import pallas as pl
from jax.experimental.pallas import tpu as pltpu
from jax.sharding import Mesh
from jax.sharding import PartitionSpec as P

E = 3072
STEPS, DEPTH = 4, 1024
SCALE = 1.0 / math.sqrt(E)
F32 = jnp.float32
BF16 = jnp.bfloat16
I32 = jnp.int32
Q = 48
K = 7
POOL = 336
X, YH, YL, Z = 4, 4, 2, 12
PEERS = YH * X
CHIPS = YL * PEERS
SLOT = 24
GROUP = 4 * Q
W = Q * PEERS
WP = W + 128
L0 = W + 7
NEG = -3.0e38
STEP = 8.0
TOP = 32700.0
TCOL, TCORE, ESCORE, EHARD = 7, 8, 9, 10


def iota(shape, dim):
    return lax.broadcasted_iota(I32, shape, dim)


def call(kernel, out, *args, flops=0, nbytes=0, mib=24, **kw):
    return pl.pallas_call(
        kernel,
        out_shape=out,
        compiler_params=pltpu.CompilerParams(vmem_limit_bytes=mib * 2**20),
        cost_estimate=pl.CostEstimate(flops=flops, bytes_accessed=nbytes, transcendentals=0),
        **kw,
    )(*args)


def dot(a, b, dims=(((1,), (0,)), ((), ()))):
    return lax.dot_general(a, b, dims, preferred_element_type=F32)


def request_kernel(place_ref, ids_ref, mine_ref, other_ref, slot_ref):
    block = jnp.concatenate([ids_ref[...], jnp.full((K, 128 - Q), -1, I32)], axis=1)
    ids = jnp.concatenate([block, jnp.full((1, 128), -1, I32)], axis=0)
    owner = lax.shift_right_arithmetic(ids * 49933, 25)
    row = ids - owner * (2 * POOL)
    high, low = lax.shift_right_arithmetic(row, 4).astype(F32), (row & 15).astype(F32)
    marks = jnp.where(owner[None] == iota((CHIPS, 8, 128), 0), 1.0, 0.0)
    flat = marks.reshape(CHIPS * 8, 128).astype(BF16)
    upper = jnp.where(iota((128, 128), 0) < iota((128, 128), 1), 1.0, 0.0).astype(BF16)
    a, b = iota((256, 256), 0), iota((256, 256), 1)
    lower = jnp.where((b < a) & (lax.shift_right_logical(a, 3) == lax.shift_right_logical(b, 3)), 1.0, 0.0).astype(BF16)
    above = dot(lower, flat).astype(BF16)
    before = dot(flat, upper) + dot(above, jnp.ones((128, 128), BF16))
    rank = jnp.sum(marks * before.reshape(CHIPS, 8, 128), axis=0)
    peer = lax.shift_right_arithmetic(owner, 3) * X + (owner & 3)
    parity = lax.shift_right_arithmetic(owner, 2) & 1
    away = parity != place_ref[2]
    cell = jnp.where(owner >= 0, peer + jnp.where(away, 2 * PEERS, 0), -1000)
    ranks = rank.T
    lanes = iota((128, 128), 1).astype(F32)
    line = iota((4 * PEERS, 128), 0)
    total = jnp.zeros((4 * PEERS, 128), F32)
    for k in range(K):
        here = cell[k : k + 1, :]
        left = jnp.where(here == line, high[k : k + 1, :], jnp.where(here + PEERS == line, low[k : k + 1, :], 0.0))
        right = jnp.where(ranks[:, k : k + 1] == lanes, 1.0, 0.0)
        total += dot(left.astype(BF16), right.astype(BF16))
    total = total.astype(BF16)
    mine_ref[...] = total[0 : 2 * PEERS]
    other_ref[...] = total[2 * PEERS :]
    slot_ref[...] = ((parity * PEERS + peer).astype(F32) * SLOT + rank).T


def passage_project_kernel(ph_ref, w_ref, out_ref):
    out_ref[...] = dot(ph_ref[...], w_ref[...]).astype(BF16)


def message_kernel(pass_ref, mine_ref, other_ref, send_ref):
    passages = pass_ref[...]
    mine, other = mine_ref[...].astype(F32), other_ref[...].astype(F32)
    line = iota((16, 128), 0)
    blank = jnp.zeros((16, 128), F32)
    for j in range(PEERS):
        part = jnp.where(
            line == 0,
            mine[j : j + 1],
            jnp.where(
                line == 1,
                mine[PEERS + j : PEERS + j + 1],
                jnp.where(line == 2, other[j : j + 1], jnp.where(line == 3, other[PEERS + j : PEERS + j + 1], 0.0)),
            ),
        )
        send_ref[j, 0:Q] = passages
        send_ref[j, Q:] = jnp.concatenate([part, blank], axis=1).astype(BF16)


def project_kernel(qh_ref, nh_ref, w_ref, pos_ref, emb_ref, acc):
    step = pl.program_id(0)

    @pl.when(step == 0)
    def _():
        acc[...] = jnp.zeros_like(acc)

    w = w_ref[...]
    acc[0:Q] += dot(qh_ref[...], w)
    acc[Q:] += dot(nh_ref[...], w)

    @pl.when(step == pl.num_programs(0) - 1)
    def _():
        emb_ref[0 : Q + POOL] = acc[...].astype(BF16)
        pos = jnp.broadcast_to(pos_ref[...], (16, 256))
        high = lax.shift_right_arithmetic(pos, 6).astype(F32)
        low = (pos & 63).astype(F32)
        emb_ref[Q + POOL :] = jnp.where(iota((16, 256), 0) == 0, high, low).astype(BF16)


def chip_kernel(place_ref, emb_ref, other_ref, chip_ref):
    first = place_ref[0] == 0

    def put(core, ref):
        chip_ref[Q * core : Q * (core + 1)] = ref[0:Q]
        chip_ref[2 * Q + 16 * core : 2 * Q + 16 * (core + 1)] = ref[Q + POOL :]

    @pl.when(first)
    def _():
        put(0, emb_ref)
        put(1, other_ref)

    @pl.when(jnp.logical_not(first))
    def _():
        put(0, other_ref)
        put(1, emb_ref)


def answer_kernel(place_ref, recv_ref, emb_ref, other_ref, send_ref, pass_ref, pool):
    core = place_ref[0]
    pool[0:POOL] = emb_ref[Q : Q + POOL]
    pool[POOL : 2 * POOL] = other_ref[Q : Q + POOL]
    pool[2 * POOL :] = jnp.zeros((768 - 2 * POOL, 256), BF16)
    pass_ref[...] = recv_ref[:, 0:Q].reshape(W, 256)
    tail = recv_ref[:, Q:].astype(F32)
    lanes = iota((SLOT, 768), 1).astype(F32)
    rows = pool[...]
    for part in range(2):
        asked = tail[:, 2 * part, 0:128] * 16.0 + tail[:, 2 * part + 1, 0:128]
        flipped = jnp.where(asked >= POOL, asked - POOL, asked + POOL)
        wanted = jnp.where(core == 1, flipped, asked).T
        base = ((place_ref[2] + part) & 1) * PEERS
        for g in range(2):
            hot = jnp.concatenate(
                [jnp.where(wanted[0:SLOT, j : j + 1] == lanes, 1.0, 0.0) for j in range(8 * g, 8 * g + 8)], axis=0
            )
            found = dot(hot.astype(BF16), rows)
            left = found[:, 0:128].reshape(8, SLOT, 128)
            right = found[:, 128:].reshape(8, SLOT, 128)
            send_ref[pl.ds(base + 8 * g, 8)] = jnp.concatenate([left, right], axis=1).astype(BF16)


def score_kernel(place_ref, chip_ref, next_ref, pass_ref, part_ref, group_ref):
    even = place_ref[2] == 0

    @pl.when(even)
    def _():
        group_ref[0 : 2 * Q] = chip_ref[0 : 2 * Q]
        group_ref[2 * Q :] = next_ref[0 : 2 * Q]

    @pl.when(jnp.logical_not(even))
    def _():
        group_ref[0 : 2 * Q] = next_ref[0 : 2 * Q]
        group_ref[2 * Q :] = chip_ref[0 : 2 * Q]

    part_ref[...] = dot(group_ref[...], pass_ref[...], (((1,), (1,)), ((), ())))


def quantize(values):
    most = jnp.maximum(jnp.max(jnp.abs(values), axis=1, keepdims=True), 1e-30)
    power = jnp.ceil(jnp.log2(most) * STEP + 0.02)
    return jnp.floor(values * (TOP * jnp.exp2(power * (-1.0 / STEP))) + 0.5), power


def hard_kernel(place_ref, part_ref, rows_ref, emb_ref, chip_ref, next_ref, slot_ref, send_ref, fetched_ref):
    parity = place_ref[2]
    got = rows_ref[...].astype(F32)
    left = got[:, 0:SLOT].reshape(CHIPS * SLOT, 128)
    right = got[:, SLOT:].reshape(CHIPS * SLOT, 128)
    rows = jnp.concatenate([left, right], axis=1).astype(BF16)
    places = iota((Q, CHIPS * SLOT), 1).astype(F32)
    slots = slot_ref[...]
    hot = jnp.concatenate([jnp.where(slots[0:Q, k : k + 1] == places, 1.0, 0.0) for k in range(K)], axis=0)
    found = dot(hot.astype(BF16), rows)
    lane = iota((Q, 128), 1)
    mine = emb_ref[0:Q].astype(F32)
    hard = jnp.zeros((Q, 128), F32)
    for k in range(K):
        row = found[Q * k : Q * (k + 1)]
        fetched_ref[k] = row.astype(BF16)
        hard = jnp.where(lane == k, jnp.sum(mine * row, axis=1, keepdims=True), hard)
    hard, power = quantize(hard)
    hard = jnp.where(lane == EHARD, power, hard)

    def target(ref, core):
        pos = ref[2 * Q + 16 * core : 2 * Q + 16 * (core + 1)].astype(F32).T
        pos = (pos[0:Q, 0:1] * 64.0 + pos[0:Q, 1:2]).astype(I32)
        index = pos.astype(F32) + 0.5
        chip = (index * (1.0 / 96.0)).astype(I32)
        dp = (index * (1.0 / 48.0)).astype(I32)
        peer = lax.shift_right_arithmetic(chip, 3) * X + (chip & 3)
        column = (peer * Q + pos - dp * Q).astype(F32)
        block = (dp - 2 * chip + 2 * (lax.shift_right_arithmetic(chip, 2) & 1)).astype(F32)
        return jnp.where(lane == TCOL, column, jnp.where(lane == TCORE, block, 0.0))

    own = 2 * parity + place_ref[0]
    scores, power = quantize(part_ref[...])
    for block in range(4):
        core = block % 2
        aim = jnp.where(parity == block // 2, target(chip_ref, core), target(next_ref, core))
        extra = aim + jnp.where(own == block, hard, 0.0)
        extra = jnp.where(lane == ESCORE, power[Q * block : Q * (block + 1)], extra)
        whole = jnp.concatenate([scores[Q * block : Q * (block + 1)], extra], axis=1)
        send_ref[3 * block : 3 * (block + 1)] = whole.reshape(3, 16, WP).astype(I32).astype(jnp.int16)


def stats_kernel(place_ref, part_ref, logit_ref, stat_ref):
    block = 2 * place_ref[2] + place_ref[0]
    z = place_ref[1]
    own = (z >= 3 * block) & (z < 3 * block + 3)
    scores = jnp.zeros((16, W), F32)
    hard = jnp.zeros((16, 128), F32)
    for i in range(Z):
        part = part_ref[i].astype(I32).astype(F32)
        extra = part[:, W:]
        scores += part[:, 0:W] * (jnp.exp2(extra[:, ESCORE : ESCORE + 1] * (1.0 / STEP)) * (SCALE / TOP))
        hard += extra * (jnp.exp2(extra[:, EHARD : EHARD + 1] * (1.0 / STEP)) * (SCALE / TOP))
    lane = iota((16, 128), 1)
    hard = jnp.where(own & (lane < K), hard, NEG)
    logits = jnp.concatenate([scores, hard], axis=1)
    peak = jnp.max(logits, axis=1, keepdims=True)
    mass = jnp.sum(jnp.where(logits > NEG, jnp.exp(logits - peak), 0.0), axis=1, keepdims=True)
    column = jnp.where(extra[:, TCORE : TCORE + 1] == block.astype(F32), extra[:, TCOL : TCOL + 1], -1.0)
    aim = iota((16, WP), 1).astype(F32) == column
    hit = jnp.sum(jnp.where(aim, logits, 0.0), axis=1, keepdims=True)
    logit_ref[...] = logits
    stat = jnp.where(
        lane == 0, peak, jnp.where(lane == 1, mass, jnp.where(lane == 2, hit, jnp.where(lane == 3, column, 0.0)))
    )
    stat_ref[...] = jnp.broadcast_to(stat[None], (4, 16, 128))


def grad_kernel(place_ref, logit_ref, stat_ref, send_ref):
    stats = [stat_ref[i] for i in range(4)]
    column = stat_ref[2 * place_ref[2] + place_ref[0]][:, 3:4]
    peak = stats[0][:, 0:1]
    for stat in stats[1:]:
        peak = jnp.maximum(peak, stat[:, 0:1])
    mass = sum(stat[:, 1:2] * jnp.exp(stat[:, 0:1] - peak) for stat in stats)
    loss = peak + jnp.log(mass) - sum(stat[:, 2:3] for stat in stats)
    logits = logit_ref[...]
    lane = iota((16, WP), 1)
    probs = jnp.where(logits > NEG, jnp.exp(logits - peak) / mass, 0.0)
    grads = probs - jnp.where(lane.astype(F32) == column, 1.0, 0.0)
    high = loss.astype(BF16).astype(F32)
    mid = (loss - high).astype(BF16).astype(F32)
    low = loss - high - mid
    grads = jnp.where(lane == L0, high, jnp.where(lane == L0 + 1, mid, jnp.where(lane == L0 + 2, low, grads)))
    send_ref[...] = jnp.broadcast_to(grads.astype(BF16)[None], (Z, 16, WP))


def turn_kernel(grad_ref, group_ref, send_ref):
    part = dot(grad_ref[:, 0:W], group_ref[...], (((0,), (0,)), ((), ())))
    send_ref[...] = part.astype(BF16).reshape(PEERS, Q, 256)


def query_kernel(place_ref, grad_ref, pass_ref, fetched_ref, emb_ref, keep_ref, give_ref, hard_ref, loss_ref, total):
    core, parity = place_ref[0], place_ref[2]
    total[...] = dot(grad_ref[:, 0:W], pass_ref[...])
    own = pl.multiple_of((2 * parity + core) * Q, 16)
    mine = grad_ref[pl.ds(own, Q), W:].astype(F32)
    queries = emb_ref[0:Q].astype(F32)
    result = total[pl.ds(own, Q)]
    for k in range(K):
        weight = mine[:, k : k + 1]
        result += weight * fetched_ref[k].astype(F32)
        hard_ref[k] = weight * queries
    total[pl.ds(own, Q)] = result
    for p in range(YL):
        keep_ref[p] = total[pl.ds(pl.multiple_of((2 * p + core) * Q, 16), Q)]
        give_ref[p] = total[pl.ds(pl.multiple_of((2 * p + 1 - core) * Q, 16), Q)]
    loss = mine[:, K : K + 1] + mine[:, K + 1 : K + 2] + mine[:, K + 2 : K + 3]
    loss_ref[...] = jnp.broadcast_to(loss, (Q, 128)).T[0:8]


def pair_kernel(place_ref, keep_ref, got_ref, mine_ref, give_ref):
    parity = place_ref[2]
    mine_ref[...] = keep_ref[parity] + got_ref[parity]
    give_ref[...] = keep_ref[1 - parity] + got_ref[1 - parity]


def passage_kernel(parts_ref, mine_ref, other_ref, out_ref, query_ref):
    total = parts_ref[0].astype(F32)
    for j in range(1, PEERS):
        total += parts_ref[j].astype(F32)
    out_ref[...] = total
    query_ref[...] = mine_ref[...] + other_ref[...]


def swap(x, axis="c"):
    return lax.ppermute(x, axis, [(0, 1), (1, 0)])


def exchange(x, axes):
    return lax.all_to_all(x, axes, split_axis=0, concat_axis=0, tiled=True)


def shape(dims, dtype):
    return jax.ShapeDtypeStruct(dims, dtype)


SMEM = pl.BlockSpec(memory_space=pltpu.SMEM)
VMEM = pl.BlockSpec(memory_space=pltpu.VMEM)


def local(query_hidden, passage_hidden, negative_hidden, projection, positive, hard_ids):
    place = jnp.stack([lax.axis_index("c"), lax.axis_index("z"), lax.axis_index("yl")]).astype(I32)
    wanted, handed, slots = call(
        request_kernel,
        (shape((2 * PEERS, 128), BF16), shape((2 * PEERS, 128), BF16), shape((128, 8), F32)),
        place,
        hard_ids.T,
        in_specs=[SMEM, VMEM],
    )
    handed = swap(handed, "yl")
    passages = call(
        passage_project_kernel,
        shape((Q, 256), BF16),
        passage_hidden,
        projection,
        flops=2 * 48 * 4096 * 256,
        nbytes=3 * 2**20,
    )
    send = call(message_kernel, shape((PEERS, Q + 16, 256), BF16), passages, wanted, handed, nbytes=2**19)
    recv = exchange(send, ("yh", "x"))

    pos = jnp.pad(positive[None, :], ((0, 0), (0, 256 - Q)))
    emb = call(
        project_kernel,
        shape((Q + POOL + 16, 256), BF16),
        query_hidden,
        negative_hidden,
        projection,
        pos,
        grid=(STEPS,),
        in_specs=[
            pl.BlockSpec((Q, DEPTH), lambda i: (0, i)),
            pl.BlockSpec((POOL, DEPTH), lambda i: (0, i)),
            pl.BlockSpec((DEPTH, 256), lambda i: (i, 0)),
            pl.BlockSpec((1, 256), lambda i: (0, 0)),
        ],
        out_specs=pl.BlockSpec((Q + POOL + 16, 256), lambda i: (0, 0)),
        scratch_shapes=[pltpu.VMEM((Q + POOL, 256), F32)],
        flops=2 * 384 * 4096 * 256,
        nbytes=6 * 2**20,
    )
    other = swap(emb)
    chip = call(
        chip_kernel,
        shape((2 * Q + 32, 256), BF16),
        place,
        emb,
        other,
        in_specs=[SMEM, VMEM, VMEM],
        nbytes=2**17,
    )
    beside = swap(chip, "yl")
    recv, emb, other, beside = lax.optimization_barrier((recv, emb, other, beside))
    answers, passages = call(
        answer_kernel,
        (shape((CHIPS, 2 * SLOT, 128), BF16), shape((W, 256), BF16)),
        place,
        recv,
        emb,
        other,
        in_specs=[SMEM] + [VMEM] * 3,
        scratch_shapes=[pltpu.VMEM((768, 256), BF16)],
        flops=2 * 768 * 768 * 256,
        nbytes=2 * 2**20,
    )
    rows = exchange(answers, ("yl", "yh", "x"))
    part, group = call(
        score_kernel,
        (shape((GROUP, W), F32), shape((GROUP, 256), BF16)),
        place,
        chip,
        beside,
        passages,
        in_specs=[SMEM] + [VMEM] * 3,
        flops=2 * 192 * 768 * 256,
        nbytes=2 * 2**20,
    )
    send, fetched = call(
        hard_kernel,
        (shape((Z, 16, WP), jnp.int16), shape((K, Q, 256), BF16)),
        place,
        part,
        rows,
        emb,
        chip,
        beside,
        slots,
        in_specs=[SMEM] + [VMEM] * 6,
        flops=2 * 336 * 768 * 256,
        nbytes=3 * 2**20,
    )
    parts = exchange(send, "z")
    logits, stat = call(
        stats_kernel,
        (shape((16, WP), F32), shape((4, 16, 128), F32)),
        place,
        parts,
        in_specs=[SMEM, VMEM],
        nbytes=2**20,
    )
    stat = exchange(stat, ("yl", "c"))
    grads = call(
        grad_kernel,
        shape((Z, 16, WP), BF16),
        place,
        logits,
        stat,
        in_specs=[SMEM, VMEM, VMEM],
        nbytes=2**19,
    )
    grads = exchange(grads, "z")
    grads = grads.reshape(GROUP, WP)
    sums = call(
        turn_kernel,
        shape((PEERS, Q, 256), BF16),
        grads,
        group,
        flops=2 * 192 * 768 * 256,
        nbytes=2 * 2**20,
    )
    sums = exchange(sums, ("yh", "x"))
    keep, give, hard_grad, loss = call(
        query_kernel,
        (shape((YL, Q, 256), F32), shape((YL, Q, 256), F32), shape((K, Q, 256), F32), shape((8, Q), F32)),
        place,
        grads,
        passages,
        fetched,
        emb,
        in_specs=[SMEM] + [VMEM] * 4,
        scratch_shapes=[pltpu.VMEM((GROUP, 256), F32)],
        flops=2 * 192 * 768 * 256,
        nbytes=3 * 2**20,
    )
    query_mine, query_give = call(
        pair_kernel,
        (shape((Q, 256), F32), shape((Q, 256), F32)),
        place,
        keep,
        swap(give),
        in_specs=[SMEM, VMEM, VMEM],
        nbytes=2**18,
    )
    passage_grad, query_grad = call(
        passage_kernel,
        (shape((Q, 256), F32), shape((Q, 256), F32)),
        sums,
        query_mine,
        swap(query_give, "yl"),
        nbytes=2**19,
    )
    return (loss[0], query_grad, passage_grad, jnp.transpose(hard_grad, (1, 0, 2)))


def solution(mesh):
    devices = np.asarray(mesh.devices)
    view = Mesh(devices.reshape(YH, YL, X, 2, Z), ("yh", "yl", "x", "c", "z"))
    dp = ("yh", "yl", "x", "c")
    return jax.shard_map(
        local,
        mesh=view,
        in_specs=(P(dp, None), P(dp, None), P(dp, None), P(None, "z"), P(dp), P(dp, None)),
        out_specs=(P(dp), P(dp, "z"), P(dp, "z"), P(dp, None, "z")),
        check_vma=False,
    )
```

```python
import math

import jax
import jax.numpy as jnp
import numpy as np
from jax import lax
from jax.experimental import pallas as pl
from jax.experimental.pallas import tpu as pltpu
from jax.sharding import Mesh
from jax.sharding import PartitionSpec as P

E = 3072
STEPS, DEPTH = 4, 1024
SCALE = 1.0 / math.sqrt(E)
F32 = jnp.float32
BF16 = jnp.bfloat16
I32 = jnp.int32
Q = 48
K = 7
POOL = 336
X, YH, YL, Z = 4, 4, 2, 12
PEERS = YH * X
CHIPS = YL * PEERS
SLOT = 24
GROUP = 4 * Q
W = Q * PEERS
WP = W + 128
L0 = W + 7
NEG = -3.0e38
STEP = 8.0
TOP = 32700.0
TCOL, TCORE, ESCORE, EHARD = 7, 8, 9, 10


def iota(shape, dim):
    return lax.broadcasted_iota(I32, shape, dim)


def call(kernel, out, *args, flops=0, nbytes=0, mib=24, **kw):
    return pl.pallas_call(
        kernel,
        out_shape=out,
        compiler_params=pltpu.CompilerParams(vmem_limit_bytes=mib * 2**20),
        cost_estimate=pl.CostEstimate(flops=flops, bytes_accessed=nbytes, transcendentals=0),
        **kw,
    )(*args)


def dot(a, b, dims=(((1,), (0,)), ((), ()))):
    return lax.dot_general(a, b, dims, preferred_element_type=F32)


def request_kernel(place_ref, ids_ref, mine_ref, other_ref, slot_ref):
    block = jnp.concatenate([ids_ref[...], jnp.full((K, 128 - Q), -1, I32)], axis=1)
    ids = jnp.concatenate([block, jnp.full((1, 128), -1, I32)], axis=0)
    owner = lax.shift_right_arithmetic(ids * 49933, 25)
    row = ids - owner * (2 * POOL)
    high, low = lax.shift_right_arithmetic(row, 4).astype(F32), (row & 15).astype(F32)
    marks = jnp.where(owner[None] == iota((CHIPS, 8, 128), 0), 1.0, 0.0)
    flat = marks.reshape(CHIPS * 8, 128).astype(BF16)
    upper = jnp.where(iota((128, 128), 0) < iota((128, 128), 1), 1.0, 0.0).astype(BF16)
    a, b = iota((256, 256), 0), iota((256, 256), 1)
    lower = jnp.where((b < a) & (lax.shift_right_logical(a, 3) == lax.shift_right_logical(b, 3)), 1.0, 0.0).astype(BF16)
    above = dot(lower, flat).astype(BF16)
    before = dot(flat, upper) + dot(above, jnp.ones((128, 128), BF16))
    rank = jnp.sum(marks * before.reshape(CHIPS, 8, 128), axis=0)
    peer = lax.shift_right_arithmetic(owner, 3) * X + (owner & 3)
    parity = lax.shift_right_arithmetic(owner, 2) & 1
    away = parity != place_ref[2]
    cell = jnp.where(owner >= 0, peer + jnp.where(away, 2 * PEERS, 0), -1000)
    ranks = rank.T
    lanes = iota((128, 128), 1).astype(F32)
    line = iota((4 * PEERS, 128), 0)
    total = jnp.zeros((4 * PEERS, 128), F32)
    for k in range(K):
        here = cell[k : k + 1, :]
        left = jnp.where(here == line, high[k : k + 1, :], jnp.where(here + PEERS == line, low[k : k + 1, :], 0.0))
        right = jnp.where(ranks[:, k : k + 1] == lanes, 1.0, 0.0)
        total += dot(left.astype(BF16), right.astype(BF16))
    total = total.astype(BF16)
    mine_ref[...] = total[0 : 2 * PEERS]
    other_ref[...] = total[2 * PEERS :]
    slot_ref[...] = ((parity * PEERS + peer).astype(F32) * SLOT + rank).T


def passage_project_kernel(ph_ref, w_ref, out_ref):
    out_ref[...] = dot(ph_ref[...], w_ref[...]).astype(BF16)


def message_kernel(pass_ref, mine_ref, other_ref, send_ref):
    passages = pass_ref[...]
    mine, other = mine_ref[...].astype(F32), other_ref[...].astype(F32)
    line = iota((16, 128), 0)
    for j in range(PEERS):
        part = jnp.where(
            line == 0,
            mine[j : j + 1],
            jnp.where(
                line == 1,
                mine[PEERS + j : PEERS + j + 1],
                jnp.where(line == 2, other[j : j + 1], jnp.where(line == 3, other[PEERS + j : PEERS + j + 1], 0.0)),
            ),
        )
        send_ref[j, 0:Q] = passages[:, 0:128]
        send_ref[j, Q : 2 * Q] = passages[:, 128:]
        send_ref[j, 2 * Q :] = part.astype(BF16)


def project_kernel(qh_ref, nh_ref, w_ref, pos_ref, emb_ref, acc):
    step = pl.program_id(0)

    @pl.when(step == 0)
    def _():
        acc[...] = jnp.zeros_like(acc)

    w = w_ref[...]
    acc[0:Q] += dot(qh_ref[...], w)
    acc[Q:] += dot(nh_ref[...], w)

    @pl.when(step == pl.num_programs(0) - 1)
    def _():
        emb_ref[0 : Q + POOL] = acc[...].astype(BF16)
        pos = jnp.broadcast_to(pos_ref[...], (16, 256))
        high = lax.shift_right_arithmetic(pos, 6).astype(F32)
        low = (pos & 63).astype(F32)
        emb_ref[Q + POOL :] = jnp.where(iota((16, 256), 0) == 0, high, low).astype(BF16)


def chip_kernel(place_ref, emb_ref, other_ref, chip_ref):
    first = place_ref[0] == 0

    def put(core, ref):
        chip_ref[Q * core : Q * (core + 1)] = ref[0:Q]
        chip_ref[2 * Q + 16 * core : 2 * Q + 16 * (core + 1)] = ref[Q + POOL :]

    @pl.when(first)
    def _():
        put(0, emb_ref)
        put(1, other_ref)

    @pl.when(jnp.logical_not(first))
    def _():
        put(0, other_ref)
        put(1, emb_ref)


def answer_kernel(place_ref, recv_ref, emb_ref, other_ref, send_ref, pool):
    core = place_ref[0]
    pool[0:POOL] = emb_ref[Q : Q + POOL]
    pool[POOL : 2 * POOL] = other_ref[Q : Q + POOL]
    pool[2 * POOL :] = jnp.zeros((768 - 2 * POOL, 256), BF16)
    tail = recv_ref[:, 2 * Q :].astype(F32)
    lanes = iota((SLOT, 768), 1).astype(F32)
    rows = pool[...]
    for part in range(2):
        asked = tail[:, 2 * part] * 16.0 + tail[:, 2 * part + 1]
        flipped = jnp.where(asked >= POOL, asked - POOL, asked + POOL)
        wanted = jnp.where(core == 1, flipped, asked).T
        base = ((place_ref[2] + part) & 1) * PEERS
        for g in range(2):
            hot = jnp.concatenate(
                [jnp.where(wanted[0:SLOT, j : j + 1] == lanes, 1.0, 0.0) for j in range(8 * g, 8 * g + 8)], axis=0
            )
            found = dot(hot.astype(BF16), rows)
            left = found[:, 0:128].reshape(8, SLOT, 128)
            right = found[:, 128:].reshape(8, SLOT, 128)
            send_ref[pl.ds(base + 8 * g, 8)] = jnp.concatenate([left, right], axis=1).astype(BF16)


def quantize(values):
    most = jnp.maximum(jnp.max(jnp.abs(values), axis=1, keepdims=True), 1e-30)
    power = jnp.ceil(jnp.log2(most) * STEP + 0.02)
    return jnp.floor(values * (TOP * jnp.exp2(power * (-1.0 / STEP))) + 0.5), power


def score_kernel(place_ref, chip_ref, next_ref, recv_ref, score_ref, extra_ref, group_ref, pass_ref):
    even = place_ref[2] == 0
    pass_ref[:, 0:128] = recv_ref[:, 0:Q].reshape(W, 128)
    pass_ref[:, 128:] = recv_ref[:, Q : 2 * Q].reshape(W, 128)

    @pl.when(even)
    def _():
        group_ref[0 : 2 * Q] = chip_ref[0 : 2 * Q]
        group_ref[2 * Q :] = next_ref[0 : 2 * Q]

    @pl.when(jnp.logical_not(even))
    def _():
        group_ref[0 : 2 * Q] = next_ref[0 : 2 * Q]
        group_ref[2 * Q :] = chip_ref[0 : 2 * Q]

    scores, power = quantize(dot(group_ref[...], pass_ref[...], (((1,), (1,)), ((), ()))))
    score_ref[...] = scores.reshape(Z, 16, W).astype(I32).astype(jnp.int16)
    lane = iota((Q, 128), 1)

    def target(ref, core):
        pos = ref[2 * Q + 16 * core : 2 * Q + 16 * (core + 1)].astype(F32).T
        pos = (pos[0:Q, 0:1] * 64.0 + pos[0:Q, 1:2]).astype(I32)
        index = pos.astype(F32) + 0.5
        chip = (index * (1.0 / 96.0)).astype(I32)
        dp = (index * (1.0 / 48.0)).astype(I32)
        peer = lax.shift_right_arithmetic(chip, 3) * X + (chip & 3)
        column = (peer * Q + pos - dp * Q).astype(F32)
        block = (dp - 2 * chip + 2 * (lax.shift_right_arithmetic(chip, 2) & 1)).astype(F32)
        return jnp.where(lane == TCOL, column, jnp.where(lane == TCORE, block, 0.0))

    for block in range(4):
        core = block % 2
        aim = jnp.where(place_ref[2] == block // 2, target(chip_ref, core), target(next_ref, core))
        extra_ref[Q * block : Q * (block + 1)] = jnp.where(lane == ESCORE, power[Q * block : Q * (block + 1)], aim)


def hard_kernel(place_ref, score_ref, extra_ref, rows_ref, emb_ref, slot_ref, send_ref, fetched_ref):
    got = rows_ref[...].astype(F32)
    left = got[:, 0:SLOT].reshape(CHIPS * SLOT, 128)
    right = got[:, SLOT:].reshape(CHIPS * SLOT, 128)
    rows = jnp.concatenate([left, right], axis=1).astype(BF16)
    places = iota((Q, CHIPS * SLOT), 1).astype(F32)
    slots = slot_ref[...]
    hot = jnp.concatenate([jnp.where(slots[0:Q, k : k + 1] == places, 1.0, 0.0) for k in range(K)], axis=0)
    found = dot(hot.astype(BF16), rows)
    lane = iota((Q, 128), 1)
    mine = emb_ref[0:Q].astype(F32)
    hard = jnp.zeros((Q, 128), F32)
    for k in range(K):
        row = found[Q * k : Q * (k + 1)]
        fetched_ref[k] = row.astype(BF16)
        hard = jnp.where(lane == k, jnp.sum(mine * row, axis=1, keepdims=True), hard)
    hard, power = quantize(hard)
    hard = jnp.where(lane == EHARD, power, hard)
    own = 2 * place_ref[2] + place_ref[0]
    send_ref[:, :, 0:W] = score_ref[...]
    for block in range(4):
        extra = extra_ref[Q * block : Q * (block + 1)] + jnp.where(own == block, hard, 0.0)
        send_ref[3 * block : 3 * (block + 1), :, W:] = extra.reshape(3, 16, 128).astype(I32).astype(jnp.int16)


def stats_kernel(place_ref, part_ref, logit_ref, stat_ref):
    block = 2 * place_ref[2] + place_ref[0]
    z = place_ref[1]
    own = (z >= 3 * block) & (z < 3 * block + 3)
    scores = jnp.zeros((16, W), F32)
    hard = jnp.zeros((16, 128), F32)
    for i in range(Z):
        part = part_ref[i].astype(I32).astype(F32)
        extra = part[:, W:]
        scores += part[:, 0:W] * (jnp.exp2(extra[:, ESCORE : ESCORE + 1] * (1.0 / STEP)) * (SCALE / TOP))
        hard += extra * (jnp.exp2(extra[:, EHARD : EHARD + 1] * (1.0 / STEP)) * (SCALE / TOP))
    lane = iota((16, 128), 1)
    hard = jnp.where(own & (lane < K), hard, NEG)
    logits = jnp.concatenate([scores, hard], axis=1)
    peak = jnp.max(logits, axis=1, keepdims=True)
    mass = jnp.sum(jnp.where(logits > NEG, jnp.exp(logits - peak), 0.0), axis=1, keepdims=True)
    column = jnp.where(extra[:, TCORE : TCORE + 1] == block.astype(F32), extra[:, TCOL : TCOL + 1], -1.0)
    aim = iota((16, WP), 1).astype(F32) == column
    hit = jnp.sum(jnp.where(aim, logits, 0.0), axis=1, keepdims=True)
    logit_ref[...] = logits
    stat = jnp.where(
        lane == 0, peak, jnp.where(lane == 1, mass, jnp.where(lane == 2, hit, jnp.where(lane == 3, column, 0.0)))
    )
    stat_ref[...] = jnp.broadcast_to(stat[None], (4, 16, 128))


def grad_kernel(place_ref, logit_ref, stat_ref, send_ref):
    stats = [stat_ref[i] for i in range(4)]
    column = stat_ref[2 * place_ref[2] + place_ref[0]][:, 3:4]
    peak = stats[0][:, 0:1]
    for stat in stats[1:]:
        peak = jnp.maximum(peak, stat[:, 0:1])
    mass = sum(stat[:, 1:2] * jnp.exp(stat[:, 0:1] - peak) for stat in stats)
    loss = peak + jnp.log(mass) - sum(stat[:, 2:3] for stat in stats)
    logits = logit_ref[...]
    lane = iota((16, WP), 1)
    probs = jnp.where(logits > NEG, jnp.exp(logits - peak) / mass, 0.0)
    grads = probs - jnp.where(lane.astype(F32) == column, 1.0, 0.0)
    high = loss.astype(BF16).astype(F32)
    mid = (loss - high).astype(BF16).astype(F32)
    low = loss - high - mid
    grads = jnp.where(lane == L0, high, jnp.where(lane == L0 + 1, mid, jnp.where(lane == L0 + 2, low, grads)))
    send_ref[...] = jnp.broadcast_to(grads.astype(BF16)[None], (Z, 16, WP))


def turn_kernel(grad_ref, group_ref, send_ref):
    part = dot(grad_ref[:, 0:W], group_ref[...], (((0,), (0,)), ((), ())))
    send_ref[...] = part.astype(BF16).reshape(PEERS, Q, 256)


def query_kernel(place_ref, grad_ref, pass_ref, fetched_ref, emb_ref, keep_ref, give_ref, hard_ref, loss_ref, total):
    core, parity = place_ref[0], place_ref[2]
    total[...] = dot(grad_ref[:, 0:W], pass_ref[...])
    own = pl.multiple_of((2 * parity + core) * Q, 16)
    mine = grad_ref[pl.ds(own, Q), W:].astype(F32)
    queries = emb_ref[0:Q].astype(F32)
    result = total[pl.ds(own, Q)]
    for k in range(K):
        weight = mine[:, k : k + 1]
        result += weight * fetched_ref[k].astype(F32)
        hard_ref[k] = weight * queries
    total[pl.ds(own, Q)] = result
    for p in range(YL):
        keep_ref[p] = total[pl.ds(pl.multiple_of((2 * p + core) * Q, 16), Q)]
        give_ref[p] = total[pl.ds(pl.multiple_of((2 * p + 1 - core) * Q, 16), Q)]
    loss = mine[:, K : K + 1] + mine[:, K + 1 : K + 2] + mine[:, K + 2 : K + 3]
    loss_ref[...] = jnp.broadcast_to(loss, (Q, 128)).T[0:8]


def pair_kernel(place_ref, keep_ref, got_ref, mine_ref, give_ref):
    parity = place_ref[2]
    mine_ref[...] = keep_ref[parity] + got_ref[parity]
    give_ref[...] = keep_ref[1 - parity] + got_ref[1 - parity]


def passage_kernel(parts_ref, mine_ref, other_ref, out_ref, query_ref):
    total = parts_ref[0].astype(F32)
    for j in range(1, PEERS):
        total += parts_ref[j].astype(F32)
    out_ref[...] = total
    query_ref[...] = mine_ref[...] + other_ref[...]


def swap(x, axis="c"):
    return lax.ppermute(x, axis, [(0, 1), (1, 0)])


def exchange(x, axes):
    return lax.all_to_all(x, axes, split_axis=0, concat_axis=0, tiled=True)


def shape(dims, dtype):
    return jax.ShapeDtypeStruct(dims, dtype)


SMEM = pl.BlockSpec(memory_space=pltpu.SMEM)
VMEM = pl.BlockSpec(memory_space=pltpu.VMEM)


def local(query_hidden, passage_hidden, negative_hidden, projection, positive, hard_ids):
    place = jnp.stack([lax.axis_index("c"), lax.axis_index("z"), lax.axis_index("yl")]).astype(I32)
    wanted, handed, slots = call(
        request_kernel,
        (shape((2 * PEERS, 128), BF16), shape((2 * PEERS, 128), BF16), shape((128, 8), F32)),
        place,
        hard_ids.T,
        in_specs=[SMEM, VMEM],
    )
    handed = swap(handed, "yl")
    passages = call(
        passage_project_kernel,
        shape((Q, 256), BF16),
        passage_hidden,
        projection,
        flops=2 * 48 * 4096 * 256,
        nbytes=3 * 2**20,
    )
    send = call(message_kernel, shape((PEERS, 2 * Q + 16, 128), BF16), passages, wanted, handed, nbytes=2**19)
    recv = exchange(send, ("yh", "x"))

    pos = jnp.pad(positive[None, :], ((0, 0), (0, 256 - Q)))
    emb = call(
        project_kernel,
        shape((Q + POOL + 16, 256), BF16),
        query_hidden,
        negative_hidden,
        projection,
        pos,
        grid=(STEPS,),
        in_specs=[
            pl.BlockSpec((Q, DEPTH), lambda i: (0, i)),
            pl.BlockSpec((POOL, DEPTH), lambda i: (0, i)),
            pl.BlockSpec((DEPTH, 256), lambda i: (i, 0)),
            pl.BlockSpec((1, 256), lambda i: (0, 0)),
        ],
        out_specs=pl.BlockSpec((Q + POOL + 16, 256), lambda i: (0, 0)),
        scratch_shapes=[pltpu.VMEM((Q + POOL, 256), F32)],
        flops=2 * 384 * 4096 * 256,
        nbytes=6 * 2**20,
    )
    other = swap(emb)
    chip = call(
        chip_kernel,
        shape((2 * Q + 32, 256), BF16),
        place,
        emb,
        other,
        in_specs=[SMEM, VMEM, VMEM],
        nbytes=2**17,
    )
    beside = swap(chip, "yl")
    recv, emb, other, beside = lax.optimization_barrier((recv, emb, other, beside))
    answers = call(
        answer_kernel,
        shape((CHIPS, 2 * SLOT, 128), BF16),
        place,
        recv,
        emb,
        other,
        in_specs=[SMEM] + [VMEM] * 3,
        scratch_shapes=[pltpu.VMEM((768, 256), BF16)],
        flops=2 * 768 * 768 * 256,
        nbytes=2 * 2**20,
    )
    rows = exchange(answers, ("yl", "yh", "x"))
    scores, extra, group, passages = call(
        score_kernel,
        (
            shape((Z, 16, W), jnp.int16),
            shape((GROUP, 128), F32),
            shape((GROUP, 256), BF16),
            shape((W, 256), BF16),
        ),
        place,
        chip,
        beside,
        recv,
        in_specs=[SMEM] + [VMEM] * 3,
        flops=2 * 192 * 768 * 256,
        nbytes=2 * 2**20,
    )
    send, fetched = call(
        hard_kernel,
        (shape((Z, 16, WP), jnp.int16), shape((K, Q, 256), BF16)),
        place,
        scores,
        extra,
        rows,
        emb,
        slots,
        in_specs=[SMEM] + [VMEM] * 5,
        flops=2 * 336 * 768 * 256,
        nbytes=2 * 2**20,
    )
    parts = exchange(send, "z")
    logits, stat = call(
        stats_kernel,
        (shape((16, WP), F32), shape((4, 16, 128), F32)),
        place,
        parts,
        in_specs=[SMEM, VMEM],
        nbytes=2**20,
    )
    stat = exchange(stat, ("yl", "c"))
    grads = call(
        grad_kernel,
        shape((Z, 16, WP), BF16),
        place,
        logits,
        stat,
        in_specs=[SMEM, VMEM, VMEM],
        nbytes=2**19,
    )
    grads = exchange(grads, "z")
    grads = grads.reshape(GROUP, WP)
    sums = call(
        turn_kernel,
        shape((PEERS, Q, 256), BF16),
        grads,
        group,
        flops=2 * 192 * 768 * 256,
        nbytes=2 * 2**20,
    )
    sums = exchange(sums, ("yh", "x"))
    keep, give, hard_grad, loss = call(
        query_kernel,
        (shape((YL, Q, 256), F32), shape((YL, Q, 256), F32), shape((K, Q, 256), F32), shape((8, Q), F32)),
        place,
        grads,
        passages,
        fetched,
        emb,
        in_specs=[SMEM] + [VMEM] * 4,
        scratch_shapes=[pltpu.VMEM((GROUP, 256), F32)],
        flops=2 * 192 * 768 * 256,
        nbytes=3 * 2**20,
    )
    query_mine, query_give = call(
        pair_kernel,
        (shape((Q, 256), F32), shape((Q, 256), F32)),
        place,
        keep,
        swap(give),
        in_specs=[SMEM, VMEM, VMEM],
        nbytes=2**18,
    )
    passage_grad, query_grad = call(
        passage_kernel,
        (shape((Q, 256), F32), shape((Q, 256), F32)),
        sums,
        query_mine,
        swap(query_give, "yl"),
        nbytes=2**19,
    )
    return (loss[0], query_grad, passage_grad, jnp.transpose(hard_grad, (1, 0, 2)))


def solution(mesh):
    devices = np.asarray(mesh.devices)
    view = Mesh(devices.reshape(YH, YL, X, 2, Z), ("yh", "yl", "x", "c", "z"))
    dp = ("yh", "yl", "x", "c")
    return jax.shard_map(
        local,
        mesh=view,
        in_specs=(P(dp, None), P(dp, None), P(dp, None), P(None, "z"), P(dp), P(dp, None)),
        out_specs=(P(dp), P(dp, "z"), P(dp, "z"), P(dp, None, "z")),
        check_vma=False,
    )
```

```python
import math

import jax
import jax.numpy as jnp
import numpy as np
from jax import lax
from jax.experimental import pallas as pl
from jax.experimental.pallas import tpu as pltpu
from jax.sharding import Mesh
from jax.sharding import PartitionSpec as P

E = 3072
STEPS, DEPTH = 4, 1024
SCALE = 1.0 / math.sqrt(E)
F32 = jnp.float32
BF16 = jnp.bfloat16
I32 = jnp.int32
Q = 48
K = 7
POOL = 336
X, YH, YL, Z = 4, 4, 2, 12
PEERS = YH * X
CHIPS = YL * PEERS
SLOT = 24
GROUP = 4 * Q
W = Q * PEERS
WP = W + 128
L0 = W + 7
NEG = -3.0e38
STEP = 8.0
TOP = 32700.0
TCOL, TCORE, ESCORE, EHARD = 7, 8, 9, 10


def iota(shape, dim):
    return lax.broadcasted_iota(I32, shape, dim)


def call(kernel, out, *args, flops=0, nbytes=0, mib=24, **kw):
    return pl.pallas_call(
        kernel,
        out_shape=out,
        compiler_params=pltpu.CompilerParams(vmem_limit_bytes=mib * 2**20),
        cost_estimate=pl.CostEstimate(flops=flops, bytes_accessed=nbytes, transcendentals=0),
        **kw,
    )(*args)


def dot(a, b, dims=(((1,), (0,)), ((), ()))):
    return lax.dot_general(a, b, dims, preferred_element_type=F32)


def request_kernel(place_ref, ids_ref, mine_ref, other_ref, slot_ref):
    block = jnp.concatenate([ids_ref[...], jnp.full((K, 128 - Q), -1, I32)], axis=1)
    ids = jnp.concatenate([block, jnp.full((1, 128), -1, I32)], axis=0)
    owner = lax.shift_right_arithmetic(ids * 49933, 25)
    row = ids - owner * (2 * POOL)
    high, low = lax.shift_right_arithmetic(row, 4).astype(F32), (row & 15).astype(F32)
    marks = jnp.where(owner[None] == iota((CHIPS, 8, 128), 0), 1.0, 0.0)
    flat = marks.reshape(CHIPS * 8, 128).astype(BF16)
    upper = jnp.where(iota((128, 128), 0) < iota((128, 128), 1), 1.0, 0.0).astype(BF16)
    a, b = iota((256, 256), 0), iota((256, 256), 1)
    lower = jnp.where((b < a) & (lax.shift_right_logical(a, 3) == lax.shift_right_logical(b, 3)), 1.0, 0.0).astype(BF16)
    above = dot(lower, flat).astype(BF16)
    before = dot(flat, upper) + dot(above, jnp.ones((128, 128), BF16))
    rank = jnp.sum(marks * before.reshape(CHIPS, 8, 128), axis=0)
    peer = lax.shift_right_arithmetic(owner, 3) * X + (owner & 3)
    parity = lax.shift_right_arithmetic(owner, 2) & 1
    away = parity != place_ref[2]
    cell = jnp.where(owner >= 0, peer + jnp.where(away, 2 * PEERS, 0), -1000)
    ranks = rank.T
    lanes = iota((128, 128), 1).astype(F32)
    line = iota((4 * PEERS, 128), 0)
    total = jnp.zeros((4 * PEERS, 128), F32)
    for k in range(K):
        here = cell[k : k + 1, :]
        left = jnp.where(here == line, high[k : k + 1, :], jnp.where(here + PEERS == line, low[k : k + 1, :], 0.0))
        right = jnp.where(ranks[:, k : k + 1] == lanes, 1.0, 0.0)
        total += dot(left.astype(BF16), right.astype(BF16))
    total = total.astype(BF16)
    mine_ref[...] = total[0 : 2 * PEERS]
    other_ref[...] = total[2 * PEERS :]
    slot_ref[...] = ((parity * PEERS + peer).astype(F32) * SLOT + rank).T


def passage_project_kernel(ph_ref, w_ref, out_ref):
    out_ref[...] = dot(ph_ref[...], w_ref[...]).astype(BF16)


def message_kernel(pass_ref, mine_ref, other_ref, send_ref):
    passages = pass_ref[...]
    mine, other = mine_ref[...].astype(F32), other_ref[...].astype(F32)
    line = iota((16, 128), 0)
    for j in range(PEERS):
        part = jnp.where(
            line == 0,
            mine[j : j + 1],
            jnp.where(
                line == 1,
                mine[PEERS + j : PEERS + j + 1],
                jnp.where(line == 2, other[j : j + 1], jnp.where(line == 3, other[PEERS + j : PEERS + j + 1], 0.0)),
            ),
        )
        send_ref[j, 0:Q] = passages[:, 0:128]
        send_ref[j, Q : 2 * Q] = passages[:, 128:]
        send_ref[j, 2 * Q :] = part.astype(BF16)


def project_kernel(qh_ref, nh_ref, w_ref, pos_ref, emb_ref, acc):
    step = pl.program_id(0)

    @pl.when(step == 0)
    def _():
        acc[...] = jnp.zeros_like(acc)

    w = w_ref[...]
    acc[0:Q] += dot(qh_ref[...], w)
    acc[Q:] += dot(nh_ref[...], w)

    @pl.when(step == pl.num_programs(0) - 1)
    def _():
        emb_ref[0 : Q + POOL] = acc[...].astype(BF16)
        pos = jnp.broadcast_to(pos_ref[...], (16, 256))
        high = lax.shift_right_arithmetic(pos, 6).astype(F32)
        low = (pos & 63).astype(F32)
        emb_ref[Q + POOL :] = jnp.where(iota((16, 256), 0) == 0, high, low).astype(BF16)


def chip_kernel(place_ref, emb_ref, other_ref, chip_ref, pool_ref):
    first = place_ref[0] == 0
    pool_ref[2 * POOL :] = jnp.zeros((768 - 2 * POOL, 256), BF16)

    def put(core, ref):
        pool_ref[POOL * core : POOL * (core + 1)] = ref[Q : Q + POOL]
        chip_ref[Q * core : Q * (core + 1)] = ref[0:Q]
        chip_ref[2 * Q + 16 * core : 2 * Q + 16 * (core + 1)] = ref[Q + POOL :]

    @pl.when(first)
    def _():
        put(0, emb_ref)
        put(1, other_ref)

    @pl.when(jnp.logical_not(first))
    def _():
        put(0, other_ref)
        put(1, emb_ref)


def answer_kernel(place_ref, recv_ref, pool_ref, send_ref):
    tail = recv_ref[:, 2 * Q :].astype(F32)
    lanes = iota((SLOT, 768), 1).astype(F32)
    rows = pool_ref[...]
    for part in range(2):
        asked = tail[:, 2 * part] * 16.0 + tail[:, 2 * part + 1]
        wanted = asked.T
        base = ((place_ref[2] + part) & 1) * PEERS
        for g in range(2):
            hot = jnp.concatenate(
                [jnp.where(wanted[0:SLOT, j : j + 1] == lanes, 1.0, 0.0) for j in range(8 * g, 8 * g + 8)], axis=0
            )
            found = dot(hot.astype(BF16), rows)
            left = found[:, 0:128].reshape(8, SLOT, 128)
            right = found[:, 128:].reshape(8, SLOT, 128)
            send_ref[pl.ds(base + 8 * g, 8)] = jnp.concatenate([left, right], axis=1).astype(BF16)


def quantize(values):
    most = jnp.maximum(jnp.max(jnp.abs(values), axis=1, keepdims=True), 1e-30)
    power = jnp.ceil(jnp.log2(most) * STEP + 0.02)
    return jnp.floor(values * (TOP * jnp.exp2(power * (-1.0 / STEP))) + 0.5), power


def score_kernel(place_ref, chip_ref, next_ref, recv_ref, slot_ref, score_ref, extra_ref, group_ref, pass_ref, hot_ref):
    places = iota((Q, CHIPS * SLOT), 1).astype(F32)
    slots = slot_ref[...]
    for k in range(K):
        hot_ref[Q * k : Q * (k + 1)] = jnp.where(slots[0:Q, k : k + 1] == places, 1.0, 0.0).astype(BF16)
    even = place_ref[2] == 0
    pass_ref[:, 0:128] = recv_ref[:, 0:Q].reshape(W, 128)
    pass_ref[:, 128:] = recv_ref[:, Q : 2 * Q].reshape(W, 128)

    @pl.when(even)
    def _():
        group_ref[0 : 2 * Q] = chip_ref[0 : 2 * Q]
        group_ref[2 * Q :] = next_ref[0 : 2 * Q]

    @pl.when(jnp.logical_not(even))
    def _():
        group_ref[0 : 2 * Q] = next_ref[0 : 2 * Q]
        group_ref[2 * Q :] = chip_ref[0 : 2 * Q]

    scores, power = quantize(dot(group_ref[...], pass_ref[...], (((1,), (1,)), ((), ()))))
    score_ref[...] = scores.reshape(Z, 16, W).astype(I32).astype(jnp.int16)
    lane = iota((Q, 128), 1)

    def target(ref, core):
        pos = ref[2 * Q + 16 * core : 2 * Q + 16 * (core + 1)].astype(F32).T
        pos = (pos[0:Q, 0:1] * 64.0 + pos[0:Q, 1:2]).astype(I32)
        index = pos.astype(F32) + 0.5
        chip = (index * (1.0 / 96.0)).astype(I32)
        dp = (index * (1.0 / 48.0)).astype(I32)
        peer = lax.shift_right_arithmetic(chip, 3) * X + (chip & 3)
        column = (peer * Q + pos - dp * Q).astype(F32)
        block = (dp - 2 * chip + 2 * (lax.shift_right_arithmetic(chip, 2) & 1)).astype(F32)
        return jnp.where(lane == TCOL, column, jnp.where(lane == TCORE, block, 0.0))

    for block in range(4):
        core = block % 2
        aim = jnp.where(place_ref[2] == block // 2, target(chip_ref, core), target(next_ref, core))
        extra_ref[Q * block : Q * (block + 1)] = jnp.where(lane == ESCORE, power[Q * block : Q * (block + 1)], aim)


def hard_kernel(place_ref, score_ref, extra_ref, rows_ref, emb_ref, hot_ref, send_ref, fetched_ref):
    got = rows_ref[...].astype(F32)
    left = got[:, 0:SLOT].reshape(CHIPS * SLOT, 128)
    right = got[:, SLOT:].reshape(CHIPS * SLOT, 128)
    rows = jnp.concatenate([left, right], axis=1).astype(BF16)
    found = dot(hot_ref[...], rows)
    lane = iota((Q, 128), 1)
    mine = emb_ref[0:Q].astype(F32)
    hard = jnp.zeros((Q, 128), F32)
    for k in range(K):
        row = found[Q * k : Q * (k + 1)]
        fetched_ref[k] = row.astype(BF16)
        hard = jnp.where(lane == k, jnp.sum(mine * row, axis=1, keepdims=True), hard)
    hard, power = quantize(hard)
    hard = jnp.where(lane == EHARD, power, hard)
    own = 2 * place_ref[2] + place_ref[0]
    send_ref[:, :, 0:W] = score_ref[...]
    for block in range(4):
        extra = extra_ref[Q * block : Q * (block + 1)] + jnp.where(own == block, hard, 0.0)
        send_ref[3 * block : 3 * (block + 1), :, W:] = extra.reshape(3, 16, 128).astype(I32).astype(jnp.int16)


def stats_kernel(place_ref, part_ref, logit_ref, stat_ref):
    block = 2 * place_ref[2] + place_ref[0]
    z = place_ref[1]
    own = (z >= 3 * block) & (z < 3 * block + 3)
    scores = jnp.zeros((16, W), F32)
    hard = jnp.zeros((16, 128), F32)
    for i in range(Z):
        part = part_ref[i].astype(I32).astype(F32)
        extra = part[:, W:]
        scores += part[:, 0:W] * (jnp.exp2(extra[:, ESCORE : ESCORE + 1] * (1.0 / STEP)) * (SCALE / TOP))
        hard += extra * (jnp.exp2(extra[:, EHARD : EHARD + 1] * (1.0 / STEP)) * (SCALE / TOP))
    lane = iota((16, 128), 1)
    hard = jnp.where(own & (lane < K), hard, NEG)
    logits = jnp.concatenate([scores, hard], axis=1)
    peak = jnp.max(logits, axis=1, keepdims=True)
    mass = jnp.sum(jnp.where(logits > NEG, jnp.exp(logits - peak), 0.0), axis=1, keepdims=True)
    column = jnp.where(extra[:, TCORE : TCORE + 1] == block.astype(F32), extra[:, TCOL : TCOL + 1], -1.0)
    aim = iota((16, WP), 1).astype(F32) == column
    hit = jnp.sum(jnp.where(aim, logits, 0.0), axis=1, keepdims=True)
    logit_ref[...] = logits
    stat = jnp.where(
        lane == 0, peak, jnp.where(lane == 1, mass, jnp.where(lane == 2, hit, jnp.where(lane == 3, column, 0.0)))
    )
    stat_ref[...] = jnp.broadcast_to(stat[None], (4, 16, 128))


def grad_kernel(place_ref, logit_ref, stat_ref, send_ref):
    stats = [stat_ref[i] for i in range(4)]
    column = stat_ref[2 * place_ref[2] + place_ref[0]][:, 3:4]
    peak = stats[0][:, 0:1]
    for stat in stats[1:]:
        peak = jnp.maximum(peak, stat[:, 0:1])
    mass = sum(stat[:, 1:2] * jnp.exp(stat[:, 0:1] - peak) for stat in stats)
    loss = peak + jnp.log(mass) - sum(stat[:, 2:3] for stat in stats)
    logits = logit_ref[...]
    lane = iota((16, WP), 1)
    probs = jnp.where(logits > NEG, jnp.exp(logits - peak) / mass, 0.0)
    grads = probs - jnp.where(lane.astype(F32) == column, 1.0, 0.0)
    high = loss.astype(BF16).astype(F32)
    mid = (loss - high).astype(BF16).astype(F32)
    low = loss - high - mid
    grads = jnp.where(lane == L0, high, jnp.where(lane == L0 + 1, mid, jnp.where(lane == L0 + 2, low, grads)))
    send_ref[...] = jnp.broadcast_to(grads.astype(BF16)[None], (Z, 16, WP))


def turn_kernel(grad_ref, group_ref, send_ref):
    part = dot(grad_ref[:, 0:W], group_ref[...], (((0,), (0,)), ((), ())))
    send_ref[...] = part.astype(BF16).reshape(PEERS, Q, 256)


def query_kernel(place_ref, grad_ref, pass_ref, fetched_ref, emb_ref, keep_ref, give_ref, hard_ref, loss_ref, total):
    core, parity = place_ref[0], place_ref[2]
    total[...] = dot(grad_ref[:, 0:W], pass_ref[...])
    own = pl.multiple_of((2 * parity + core) * Q, 16)
    mine = grad_ref[pl.ds(own, Q), W:].astype(F32)
    queries = emb_ref[0:Q].astype(F32)
    result = total[pl.ds(own, Q)]
    for k in range(K):
        weight = mine[:, k : k + 1]
        result += weight * fetched_ref[k].astype(F32)
        hard_ref[k] = weight * queries
    total[pl.ds(own, Q)] = result
    for p in range(YL):
        keep_ref[p] = total[pl.ds(pl.multiple_of((2 * p + core) * Q, 16), Q)]
        give_ref[p] = total[pl.ds(pl.multiple_of((2 * p + 1 - core) * Q, 16), Q)].astype(BF16)
    loss = mine[:, K : K + 1] + mine[:, K + 1 : K + 2] + mine[:, K + 2 : K + 3]
    loss_ref[...] = jnp.broadcast_to(loss, (Q, 128)).T[0:8]


def pair_kernel(place_ref, keep_ref, got_ref, mine_ref, give_ref):
    parity = place_ref[2]
    mine_ref[...] = keep_ref[parity] + got_ref[parity].astype(F32)
    give_ref[...] = (keep_ref[1 - parity] + got_ref[1 - parity].astype(F32)).astype(BF16)


def passage_kernel(parts_ref, mine_ref, other_ref, out_ref, query_ref):
    total = parts_ref[0].astype(F32)
    for j in range(1, PEERS):
        total += parts_ref[j].astype(F32)
    out_ref[...] = total
    query_ref[...] = mine_ref[...] + other_ref[...].astype(F32)


def swap(x, axis="c"):
    return lax.ppermute(x, axis, [(0, 1), (1, 0)])


def exchange(x, axes):
    return lax.all_to_all(x, axes, split_axis=0, concat_axis=0, tiled=True)


def shape(dims, dtype):
    return jax.ShapeDtypeStruct(dims, dtype)


SMEM = pl.BlockSpec(memory_space=pltpu.SMEM)
VMEM = pl.BlockSpec(memory_space=pltpu.VMEM)


def local(query_hidden, passage_hidden, negative_hidden, projection, positive, hard_ids):
    place = jnp.stack([lax.axis_index("c"), lax.axis_index("z"), lax.axis_index("yl")]).astype(I32)
    wanted, handed, slots = call(
        request_kernel,
        (shape((2 * PEERS, 128), BF16), shape((2 * PEERS, 128), BF16), shape((128, 8), F32)),
        place,
        hard_ids.T,
        in_specs=[SMEM, VMEM],
    )
    handed = swap(handed, "yl")
    passages = call(
        passage_project_kernel,
        shape((Q, 256), BF16),
        passage_hidden,
        projection,
        flops=2 * 48 * 4096 * 256,
        nbytes=3 * 2**20,
    )
    send = call(message_kernel, shape((PEERS, 2 * Q + 16, 128), BF16), passages, wanted, handed, nbytes=2**19)
    recv = exchange(send, ("yh", "x"))

    pos = jnp.pad(positive[None, :], ((0, 0), (0, 256 - Q)))
    emb = call(
        project_kernel,
        shape((Q + POOL + 16, 256), BF16),
        query_hidden,
        negative_hidden,
        projection,
        pos,
        grid=(STEPS,),
        in_specs=[
            pl.BlockSpec((Q, DEPTH), lambda i: (0, i)),
            pl.BlockSpec((POOL, DEPTH), lambda i: (0, i)),
            pl.BlockSpec((DEPTH, 256), lambda i: (i, 0)),
            pl.BlockSpec((1, 256), lambda i: (0, 0)),
        ],
        out_specs=pl.BlockSpec((Q + POOL + 16, 256), lambda i: (0, 0)),
        scratch_shapes=[pltpu.VMEM((Q + POOL, 256), F32)],
        flops=2 * 384 * 4096 * 256,
        nbytes=6 * 2**20,
    )
    other = swap(emb)
    chip, pool = call(
        chip_kernel,
        (shape((2 * Q + 32, 256), BF16), shape((768, 256), BF16)),
        place,
        emb,
        other,
        in_specs=[SMEM, VMEM, VMEM],
        nbytes=2**17,
    )
    beside = swap(chip, "yl")
    recv, pool, beside = lax.optimization_barrier((recv, pool, beside))
    answers = call(
        answer_kernel,
        shape((CHIPS, 2 * SLOT, 128), BF16),
        place,
        recv,
        pool,
        in_specs=[SMEM] + [VMEM] * 2,
        flops=2 * 768 * 768 * 256,
        nbytes=2 * 2**20,
    )
    rows = exchange(answers, ("yl", "yh", "x"))
    scores, extra, group, passages, hot = call(
        score_kernel,
        (
            shape((Z, 16, W), jnp.int16),
            shape((GROUP, 128), F32),
            shape((GROUP, 256), BF16),
            shape((W, 256), BF16),
            shape((K * Q, CHIPS * SLOT), BF16),
        ),
        place,
        chip,
        beside,
        recv,
        slots,
        in_specs=[SMEM] + [VMEM] * 4,
        flops=2 * 192 * 768 * 256,
        nbytes=2 * 2**20,
    )
    send, fetched = call(
        hard_kernel,
        (shape((Z, 16, WP), jnp.int16), shape((K, Q, 256), BF16)),
        place,
        scores,
        extra,
        rows,
        emb,
        hot,
        in_specs=[SMEM] + [VMEM] * 5,
        flops=2 * 336 * 768 * 256,
        nbytes=2 * 2**20,
    )
    parts = exchange(send, "z")
    logits, stat = call(
        stats_kernel,
        (shape((16, WP), F32), shape((4, 16, 128), F32)),
        place,
        parts,
        in_specs=[SMEM, VMEM],
        nbytes=2**20,
    )
    stat = exchange(stat, ("yl", "c"))
    grads = call(
        grad_kernel,
        shape((Z, 16, WP), BF16),
        place,
        logits,
        stat,
        in_specs=[SMEM, VMEM, VMEM],
        nbytes=2**19,
    )
    grads = exchange(grads, "z")
    grads = grads.reshape(GROUP, WP)
    sums = call(
        turn_kernel,
        shape((PEERS, Q, 256), BF16),
        grads,
        group,
        flops=2 * 192 * 768 * 256,
        nbytes=2 * 2**20,
    )
    sums = exchange(sums, ("yh", "x"))
    keep, give, hard_grad, loss = call(
        query_kernel,
        (shape((YL, Q, 256), F32), shape((YL, Q, 256), BF16), shape((K, Q, 256), F32), shape((8, Q), F32)),
        place,
        grads,
        passages,
        fetched,
        emb,
        in_specs=[SMEM] + [VMEM] * 4,
        scratch_shapes=[pltpu.VMEM((GROUP, 256), F32)],
        flops=2 * 192 * 768 * 256,
        nbytes=3 * 2**20,
    )
    query_mine, query_give = call(
        pair_kernel,
        (shape((Q, 256), F32), shape((Q, 256), BF16)),
        place,
        keep,
        swap(give),
        in_specs=[SMEM, VMEM, VMEM],
        nbytes=2**18,
    )
    passage_grad, query_grad = call(
        passage_kernel,
        (shape((Q, 256), F32), shape((Q, 256), F32)),
        sums,
        query_mine,
        swap(query_give, "yl"),
        nbytes=2**19,
    )
    return (loss[0], query_grad, passage_grad, jnp.transpose(hard_grad, (1, 0, 2)))


def solution(mesh):
    devices = np.asarray(mesh.devices)
    view = Mesh(devices.reshape(YH, YL, X, 2, Z), ("yh", "yl", "x", "c", "z"))
    dp = ("yh", "yl", "x", "c")
    return jax.shard_map(
        local,
        mesh=view,
        in_specs=(P(dp, None), P(dp, None), P(dp, None), P(None, "z"), P(dp), P(dp, None)),
        out_specs=(P(dp), P(dp, "z"), P(dp, "z"), P(dp, None, "z")),
        check_vma=False,
    )
```

```python
import math

import jax
import jax.numpy as jnp
import numpy as np
from jax import lax
from jax.experimental import pallas as pl
from jax.experimental.pallas import tpu as pltpu
from jax.sharding import Mesh
from jax.sharding import PartitionSpec as P

E = 3072
STEPS, DEPTH = 4, 1024
SCALE = 1.0 / math.sqrt(E)
F32 = jnp.float32
BF16 = jnp.bfloat16
I32 = jnp.int32
Q = 48
K = 7
POOL = 336
X, YH, YL, Z = 4, 4, 2, 12
PEERS = YH * X
CHIPS = YL * PEERS
SLOT = 24
GROUP = 4 * Q
W = Q * PEERS
WP = W + 128
L0 = W + 7
NEG = -3.0e38
STEP = 8.0
TOP = 32700.0
TCOL, TCORE, ESCORE, EHARD = 7, 8, 9, 10


def iota(shape, dim):
    return lax.broadcasted_iota(I32, shape, dim)


def call(kernel, out, *args, flops=0, nbytes=0, mib=24, **kw):
    return pl.pallas_call(
        kernel,
        out_shape=out,
        compiler_params=pltpu.CompilerParams(vmem_limit_bytes=mib * 2**20),
        cost_estimate=pl.CostEstimate(flops=flops, bytes_accessed=nbytes, transcendentals=0),
        **kw,
    )(*args)


def dot(a, b, dims=(((1,), (0,)), ((), ()))):
    return lax.dot_general(a, b, dims, preferred_element_type=F32)


def request_kernel(place_ref, ids_ref, mine_ref, other_ref, slot_ref):
    block = jnp.concatenate([ids_ref[...], jnp.full((K, 128 - Q), -1, I32)], axis=1)
    ids = jnp.concatenate([block, jnp.full((1, 128), -1, I32)], axis=0)
    owner = lax.shift_right_arithmetic(ids * 49933, 25)
    row = ids - owner * (2 * POOL)
    high, low = lax.shift_right_arithmetic(row, 4).astype(F32), (row & 15).astype(F32)
    marks = jnp.where(owner[None] == iota((CHIPS, 8, 128), 0), 1.0, 0.0)
    flat = marks.reshape(CHIPS * 8, 128).astype(BF16)
    upper = jnp.where(iota((128, 128), 0) < iota((128, 128), 1), 1.0, 0.0).astype(BF16)
    a, b = iota((256, 256), 0), iota((256, 256), 1)
    lower = jnp.where((b < a) & (lax.shift_right_logical(a, 3) == lax.shift_right_logical(b, 3)), 1.0, 0.0).astype(BF16)
    above = dot(lower, flat).astype(BF16)
    before = dot(flat, upper) + dot(above, jnp.ones((128, 128), BF16))
    rank = jnp.sum(marks * before.reshape(CHIPS, 8, 128), axis=0)
    peer = lax.shift_right_arithmetic(owner, 3) * X + (owner & 3)
    parity = lax.shift_right_arithmetic(owner, 2) & 1
    away = parity != place_ref[2]
    cell = jnp.where(owner >= 0, peer + jnp.where(away, 2 * PEERS, 0), -1000)
    ranks = rank.T
    lanes = iota((128, 128), 1).astype(F32)
    line = iota((4 * PEERS, 128), 0)
    total = jnp.zeros((4 * PEERS, 128), F32)
    for k in range(K):
        here = cell[k : k + 1, :]
        left = jnp.where(here == line, high[k : k + 1, :], jnp.where(here + PEERS == line, low[k : k + 1, :], 0.0))
        right = jnp.where(ranks[:, k : k + 1] == lanes, 1.0, 0.0)
        total += dot(left.astype(BF16), right.astype(BF16))
    total = total.astype(BF16)
    mine_ref[...] = total[0 : 2 * PEERS]
    other_ref[...] = total[2 * PEERS :]
    slot_ref[...] = ((parity * PEERS + peer).astype(F32) * SLOT + rank).T


def passage_project_kernel(ph_ref, w_ref, out_ref):
    out_ref[...] = dot(ph_ref[...], w_ref[...]).astype(BF16)


def message_kernel(pass_ref, mine_ref, other_ref, send_ref):
    passages = pass_ref[...]
    mine, other = mine_ref[...].astype(F32), other_ref[...].astype(F32)
    line = iota((16, 128), 0)
    for j in range(PEERS):
        part = jnp.where(
            line == 0,
            mine[j : j + 1],
            jnp.where(
                line == 1,
                mine[PEERS + j : PEERS + j + 1],
                jnp.where(line == 2, other[j : j + 1], jnp.where(line == 3, other[PEERS + j : PEERS + j + 1], 0.0)),
            ),
        )
        send_ref[j, 0:Q] = passages[:, 0:128]
        send_ref[j, Q : 2 * Q] = passages[:, 128:]
        send_ref[j, 2 * Q :] = part.astype(BF16)


def project_kernel(qh_ref, nh_ref, w_ref, pos_ref, emb_ref, acc):
    step = pl.program_id(0)

    @pl.when(step == 0)
    def _():
        acc[...] = jnp.zeros_like(acc)

    w = w_ref[...]
    acc[0:Q] += dot(qh_ref[...], w)
    acc[Q:] += dot(nh_ref[...], w)

    @pl.when(step == pl.num_programs(0) - 1)
    def _():
        emb_ref[0 : Q + POOL] = acc[...].astype(BF16)
        pos = jnp.broadcast_to(pos_ref[...], (16, 256))
        high = lax.shift_right_arithmetic(pos, 6).astype(F32)
        low = (pos & 63).astype(F32)
        emb_ref[Q + POOL :] = jnp.where(iota((16, 256), 0) == 0, high, low).astype(BF16)


def chip_kernel(place_ref, emb_ref, other_ref, chip_ref):
    first = place_ref[0] == 0

    def put(core, ref):
        chip_ref[Q * core : Q * (core + 1)] = ref[0:Q]
        chip_ref[2 * Q + 16 * core : 2 * Q + 16 * (core + 1)] = ref[Q + POOL :]

    @pl.when(first)
    def _():
        put(0, emb_ref)
        put(1, other_ref)

    @pl.when(jnp.logical_not(first))
    def _():
        put(0, other_ref)
        put(1, emb_ref)


def answer_kernel(place_ref, recv_ref, emb_ref, other_ref, send_ref, pool):
    core = place_ref[0]
    pool[0:POOL] = emb_ref[Q : Q + POOL]
    pool[POOL : 2 * POOL] = other_ref[Q : Q + POOL]
    pool[2 * POOL :] = jnp.zeros((768 - 2 * POOL, 256), BF16)
    tail = recv_ref[:, 2 * Q :].astype(F32)
    lanes = iota((SLOT, 768), 1).astype(F32)
    rows = pool[...]
    for part in range(2):
        asked = tail[:, 2 * part] * 16.0 + tail[:, 2 * part + 1]
        flipped = jnp.where(asked >= POOL, asked - POOL, asked + POOL)
        wanted = jnp.where(core == 1, flipped, asked).T
        base = ((place_ref[2] + part) & 1) * PEERS
        for g in range(2):
            hot = jnp.concatenate(
                [jnp.where(wanted[0:SLOT, j : j + 1] == lanes, 1.0, 0.0) for j in range(8 * g, 8 * g + 8)], axis=0
            )
            found = dot(hot.astype(BF16), rows)
            left = found[:, 0:128].reshape(8, SLOT, 128)
            right = found[:, 128:].reshape(8, SLOT, 128)
            send_ref[pl.ds(base + 8 * g, 8)] = jnp.concatenate([left, right], axis=1).astype(BF16)


def quantize(values):
    most = jnp.maximum(jnp.max(jnp.abs(values), axis=1, keepdims=True), 1e-30)
    power = jnp.ceil(jnp.log2(most) * STEP + 0.02)
    return jnp.floor(values * (TOP * jnp.exp2(power * (-1.0 / STEP))) + 0.5), power


def score_kernel(place_ref, chip_ref, next_ref, recv_ref, score_ref, extra_ref, group_ref, pass_ref):
    even = place_ref[2] == 0
    pass_ref[:, 0:128] = recv_ref[:, 0:Q].reshape(W, 128)
    pass_ref[:, 128:] = recv_ref[:, Q : 2 * Q].reshape(W, 128)

    @pl.when(even)
    def _():
        group_ref[0 : 2 * Q] = chip_ref[0 : 2 * Q]
        group_ref[2 * Q :] = next_ref[0 : 2 * Q]

    @pl.when(jnp.logical_not(even))
    def _():
        group_ref[0 : 2 * Q] = next_ref[0 : 2 * Q]
        group_ref[2 * Q :] = chip_ref[0 : 2 * Q]

    scores, power = quantize(dot(group_ref[...], pass_ref[...], (((1,), (1,)), ((), ()))))
    score_ref[...] = scores.reshape(Z, 16, W).astype(I32).astype(jnp.int16)
    lane = iota((Q, 128), 1)

    def target(ref, core):
        pos = ref[2 * Q + 16 * core : 2 * Q + 16 * (core + 1)].astype(F32).T
        pos = (pos[0:Q, 0:1] * 64.0 + pos[0:Q, 1:2]).astype(I32)
        index = pos.astype(F32) + 0.5
        chip = (index * (1.0 / 96.0)).astype(I32)
        dp = (index * (1.0 / 48.0)).astype(I32)
        peer = lax.shift_right_arithmetic(chip, 3) * X + (chip & 3)
        column = (peer * Q + pos - dp * Q).astype(F32)
        block = (dp - 2 * chip + 2 * (lax.shift_right_arithmetic(chip, 2) & 1)).astype(F32)
        return jnp.where(lane == TCOL, column, jnp.where(lane == TCORE, block, 0.0))

    for block in range(4):
        core = block % 2
        aim = jnp.where(place_ref[2] == block // 2, target(chip_ref, core), target(next_ref, core))
        extra_ref[Q * block : Q * (block + 1)] = jnp.where(lane == ESCORE, power[Q * block : Q * (block + 1)], aim)


def hard_kernel(place_ref, score_ref, extra_ref, rows_ref, emb_ref, slot_ref, send_ref, fetched_ref):
    got = rows_ref[...].astype(F32)
    left = got[:, 0:SLOT].reshape(CHIPS * SLOT, 128)
    right = got[:, SLOT:].reshape(CHIPS * SLOT, 128)
    rows = jnp.concatenate([left, right], axis=1).astype(BF16)
    places = iota((Q, CHIPS * SLOT), 1).astype(F32)
    slots = slot_ref[...]
    hot = jnp.concatenate([jnp.where(slots[0:Q, k : k + 1] == places, 1.0, 0.0) for k in range(K)], axis=0)
    found = dot(hot.astype(BF16), rows)
    lane = iota((Q, 128), 1)
    mine = emb_ref[0:Q].astype(F32)
    hard = jnp.zeros((Q, 128), F32)
    for k in range(K):
        row = found[Q * k : Q * (k + 1)]
        fetched_ref[k] = row.astype(BF16)
        hard = jnp.where(lane == k, jnp.sum(mine * row, axis=1, keepdims=True), hard)
    hard, power = quantize(hard)
    hard = jnp.where(lane == EHARD, power, hard)
    own = 2 * place_ref[2] + place_ref[0]
    send_ref[:, :, 0:W] = score_ref[...]
    for block in range(4):
        extra = extra_ref[Q * block : Q * (block + 1)] + jnp.where(own == block, hard, 0.0)
        send_ref[3 * block : 3 * (block + 1), :, W:] = extra.reshape(3, 16, 128).astype(I32).astype(jnp.int16)


def stats_kernel(place_ref, part_ref, logit_ref, stat_ref):
    block = 2 * place_ref[2] + place_ref[0]
    z = place_ref[1]
    own = (z >= 3 * block) & (z < 3 * block + 3)
    scores = jnp.zeros((16, W), F32)
    hard = jnp.zeros((16, 128), F32)
    for i in range(Z):
        part = part_ref[i].astype(I32).astype(F32)
        extra = part[:, W:]
        scores += part[:, 0:W] * (jnp.exp2(extra[:, ESCORE : ESCORE + 1] * (1.0 / STEP)) * (SCALE / TOP))
        hard += extra * (jnp.exp2(extra[:, EHARD : EHARD + 1] * (1.0 / STEP)) * (SCALE / TOP))
    lane = iota((16, 128), 1)
    hard = jnp.where(own & (lane < K), hard, NEG)
    logits = jnp.concatenate([scores, hard], axis=1)
    peak = jnp.max(logits, axis=1, keepdims=True)
    mass = jnp.sum(jnp.where(logits > NEG, jnp.exp(logits - peak), 0.0), axis=1, keepdims=True)
    column = jnp.where(extra[:, TCORE : TCORE + 1] == block.astype(F32), extra[:, TCOL : TCOL + 1], -1.0)
    aim = iota((16, WP), 1).astype(F32) == column
    hit = jnp.sum(jnp.where(aim, logits, 0.0), axis=1, keepdims=True)
    logit_ref[...] = logits
    stat = jnp.where(
        lane == 0, peak, jnp.where(lane == 1, mass, jnp.where(lane == 2, hit, jnp.where(lane == 3, column, 0.0)))
    )
    stat_ref[...] = jnp.broadcast_to(stat[None], (4, 16, 128))


def grad_kernel(place_ref, logit_ref, stat_ref, send_ref):
    stats = [stat_ref[i] for i in range(4)]
    column = stat_ref[2 * place_ref[2] + place_ref[0]][:, 3:4]
    peak = stats[0][:, 0:1]
    for stat in stats[1:]:
        peak = jnp.maximum(peak, stat[:, 0:1])
    mass = sum(stat[:, 1:2] * jnp.exp(stat[:, 0:1] - peak) for stat in stats)
    loss = peak + jnp.log(mass) - sum(stat[:, 2:3] for stat in stats)
    logits = logit_ref[...]
    lane = iota((16, WP), 1)
    probs = jnp.where(logits > NEG, jnp.exp(logits - peak) / mass, 0.0)
    grads = probs - jnp.where(lane.astype(F32) == column, 1.0, 0.0)
    high = loss.astype(BF16).astype(F32)
    mid = (loss - high).astype(BF16).astype(F32)
    low = loss - high - mid
    grads = jnp.where(lane == L0, high, jnp.where(lane == L0 + 1, mid, jnp.where(lane == L0 + 2, low, grads)))
    send_ref[...] = jnp.broadcast_to(grads.astype(BF16)[None], (Z, 16, WP))


def turn_kernel(grad_ref, group_ref, send_ref):
    part = dot(grad_ref[:, 0:W], group_ref[...], (((0,), (0,)), ((), ())))
    send_ref[...] = part.astype(BF16).reshape(PEERS, Q, 256)


def query_kernel(place_ref, grad_ref, pass_ref, fetched_ref, emb_ref, keep_ref, give_ref, hard_ref, loss_ref, total):
    core, parity = place_ref[0], place_ref[2]
    total[...] = dot(grad_ref[:, 0:W], pass_ref[...])
    own = pl.multiple_of((2 * parity + core) * Q, 16)
    mine = grad_ref[pl.ds(own, Q), W:].astype(F32)
    queries = emb_ref[0:Q].astype(F32)
    result = total[pl.ds(own, Q)]
    for k in range(K):
        weight = mine[:, k : k + 1]
        result += weight * fetched_ref[k].astype(F32)
        hard_ref[k] = weight * queries
    total[pl.ds(own, Q)] = result
    for p in range(YL):
        keep_ref[p] = total[pl.ds(pl.multiple_of((2 * p + core) * Q, 16), Q)]
        give_ref[p] = total[pl.ds(pl.multiple_of((2 * p + 1 - core) * Q, 16), Q)]
    loss = mine[:, K : K + 1] + mine[:, K + 1 : K + 2] + mine[:, K + 2 : K + 3]
    loss_ref[...] = jnp.broadcast_to(loss, (Q, 128)).T[0:8]


def pair_kernel(place_ref, keep_ref, got_ref, mine_ref, give_ref):
    parity = place_ref[2]
    mine_ref[...] = keep_ref[parity] + got_ref[parity]
    give_ref[...] = keep_ref[1 - parity] + got_ref[1 - parity]


def passage_kernel(parts_ref, mine_ref, other_ref, out_ref, query_ref):
    total = parts_ref[0].astype(F32)
    for j in range(1, PEERS):
        total += parts_ref[j].astype(F32)
    out_ref[...] = total
    query_ref[...] = mine_ref[...] + other_ref[...]


def swap(x, axis="c"):
    return lax.ppermute(x, axis, [(0, 1), (1, 0)])


def exchange(x, axes):
    return lax.all_to_all(x, axes, split_axis=0, concat_axis=0, tiled=True)


def shape(dims, dtype):
    return jax.ShapeDtypeStruct(dims, dtype)


SMEM = pl.BlockSpec(memory_space=pltpu.SMEM)
VMEM = pl.BlockSpec(memory_space=pltpu.VMEM)


def local(query_hidden, passage_hidden, negative_hidden, projection, positive, hard_ids):
    place = jnp.stack([lax.axis_index("c"), lax.axis_index("z"), lax.axis_index("yl")]).astype(I32)
    wanted, handed, slots = call(
        request_kernel,
        (shape((2 * PEERS, 128), BF16), shape((2 * PEERS, 128), BF16), shape((128, 8), F32)),
        place,
        hard_ids.T,
        in_specs=[SMEM, VMEM],
    )
    handed = swap(handed, "yl")
    passages = call(
        passage_project_kernel,
        shape((Q, 256), BF16),
        passage_hidden,
        projection,
        flops=2 * 48 * 4096 * 256,
        nbytes=3 * 2**20,
    )
    send = call(message_kernel, shape((PEERS, 2 * Q + 16, 128), BF16), passages, wanted, handed, nbytes=2**19)
    recv = exchange(send, ("yh", "x"))

    pos = jnp.pad(positive[None, :], ((0, 0), (0, 256 - Q)))
    emb = call(
        project_kernel,
        shape((Q + POOL + 16, 256), BF16),
        query_hidden,
        negative_hidden,
        projection,
        pos,
        grid=(STEPS,),
        in_specs=[
            pl.BlockSpec((Q, DEPTH), lambda i: (0, i)),
            pl.BlockSpec((POOL, DEPTH), lambda i: (0, i)),
            pl.BlockSpec((DEPTH, 256), lambda i: (i, 0)),
            pl.BlockSpec((1, 256), lambda i: (0, 0)),
        ],
        out_specs=pl.BlockSpec((Q + POOL + 16, 256), lambda i: (0, 0)),
        scratch_shapes=[pltpu.VMEM((Q + POOL, 256), F32)],
        flops=2 * 384 * 4096 * 256,
        nbytes=6 * 2**20,
    )
    other = swap(emb)
    chip = call(
        chip_kernel,
        shape((2 * Q + 32, 256), BF16),
        place,
        emb,
        other,
        in_specs=[SMEM, VMEM, VMEM],
        nbytes=2**17,
    )
    recv, emb, other, chip = lax.optimization_barrier((recv, emb, other, chip))
    beside = swap(chip, "yl")
    answers = call(
        answer_kernel,
        shape((CHIPS, 2 * SLOT, 128), BF16),
        place,
        recv,
        emb,
        other,
        in_specs=[SMEM] + [VMEM] * 3,
        scratch_shapes=[pltpu.VMEM((768, 256), BF16)],
        flops=2 * 768 * 768 * 256,
        nbytes=2 * 2**20,
    )
    rows = exchange(answers, ("yl", "yh", "x"))
    scores, extra, group, passages = call(
        score_kernel,
        (
            shape((Z, 16, W), jnp.int16),
            shape((GROUP, 128), F32),
            shape((GROUP, 256), BF16),
            shape((W, 256), BF16),
        ),
        place,
        chip,
        beside,
        recv,
        in_specs=[SMEM] + [VMEM] * 3,
        flops=2 * 192 * 768 * 256,
        nbytes=2 * 2**20,
    )
    send, fetched = call(
        hard_kernel,
        (shape((Z, 16, WP), jnp.int16), shape((K, Q, 256), BF16)),
        place,
        scores,
        extra,
        rows,
        emb,
        slots,
        in_specs=[SMEM] + [VMEM] * 5,
        flops=2 * 336 * 768 * 256,
        nbytes=2 * 2**20,
    )
    parts = exchange(send, "z")
    logits, stat = call(
        stats_kernel,
        (shape((16, WP), F32), shape((4, 16, 128), F32)),
        place,
        parts,
        in_specs=[SMEM, VMEM],
        nbytes=2**20,
    )
    stat = exchange(stat, ("yl", "c"))
    grads = call(
        grad_kernel,
        shape((Z, 16, WP), BF16),
        place,
        logits,
        stat,
        in_specs=[SMEM, VMEM, VMEM],
        nbytes=2**19,
    )
    grads = exchange(grads, "z")
    grads = grads.reshape(GROUP, WP)
    sums = call(
        turn_kernel,
        shape((PEERS, Q, 256), BF16),
        grads,
        group,
        flops=2 * 192 * 768 * 256,
        nbytes=2 * 2**20,
    )
    sums = exchange(sums, ("yh", "x"))
    keep, give, hard_grad, loss = call(
        query_kernel,
        (shape((YL, Q, 256), F32), shape((YL, Q, 256), F32), shape((K, Q, 256), F32), shape((8, Q), F32)),
        place,
        grads,
        passages,
        fetched,
        emb,
        in_specs=[SMEM] + [VMEM] * 4,
        scratch_shapes=[pltpu.VMEM((GROUP, 256), F32)],
        flops=2 * 192 * 768 * 256,
        nbytes=3 * 2**20,
    )
    query_mine, query_give = call(
        pair_kernel,
        (shape((Q, 256), F32), shape((Q, 256), F32)),
        place,
        keep,
        swap(give),
        in_specs=[SMEM, VMEM, VMEM],
        nbytes=2**18,
    )
    passage_grad, query_grad = call(
        passage_kernel,
        (shape((Q, 256), F32), shape((Q, 256), F32)),
        sums,
        query_mine,
        swap(query_give, "yl"),
        nbytes=2**19,
    )
    return (loss[0], query_grad, passage_grad, jnp.transpose(hard_grad, (1, 0, 2)))


def solution(mesh):
    devices = np.asarray(mesh.devices)
    view = Mesh(devices.reshape(YH, YL, X, 2, Z), ("yh", "yl", "x", "c", "z"))
    dp = ("yh", "yl", "x", "c")
    return jax.shard_map(
        local,
        mesh=view,
        in_specs=(P(dp, None), P(dp, None), P(dp, None), P(None, "z"), P(dp), P(dp, None)),
        out_specs=(P(dp), P(dp, "z"), P(dp, "z"), P(dp, None, "z")),
        check_vma=False,
    )
```
